256 devices in a mesh: seq: 32 (over x, z), exp: 8 (over y, core).
Axes of the slice: x: 4, y: 4, z: 8, core: 2. Of those that a mesh axis runs over, the one named last changes fastest.
Arguments:
- queries: bfloat16 [4096, 4096], P('seq', 'exp'), may hold values from -2 to 2
- keys: bfloat16 [4096, 4096], P('seq', 'exp'), may hold values from -2 to 2
- values: bfloat16 [4096, 4096], P('seq', 'exp'), may hold values from -6 to 6
- log_decay: float32 [4096, 32], P('seq', 'exp'), may hold values from -1 to 0, as said below
- residual: bfloat16 [4096, 4096], P(('seq', 'exp')), may hold values from -6 to 6
- attn_gain: float32 [4096], replicated, may hold values from 0.25 to 1.75
- moe_gain: float32 [4096], replicated, may hold values from 0.25 to 1.75
- expert_ids: int32 [4096, 2], P(('seq', 'exp')), may hold values from 0 to 7, all different within a row; in each aligned block of 16 rows (0 to 15, 16 to 31, ...) at most 6 rows name the same one
- gate_weights: float32 [4096, 2], P(('seq', 'exp')), may hold values from 0.2 to 1
- w_gate: bfloat16 [8, 9216, 4096], P('exp', 'seq'), may hold values from -0.09375 to 0.09375
- w_up: bfloat16 [8, 9216, 4096], P('exp', 'seq'), may hold values from -0.09375 to 0.09375
- w_down: bfloat16 [8, 9216, 4096], P('exp', 'seq'), may hold values from -0.0625 to 0.0625
Outputs:
- layer_out: bfloat16 [4096, 4096], P(('seq', 'exp'))
The draws below stay inside these ranges and needn't reach their ends.
Inputs may be any that keep to these rules, and one draw needn't show every extreme that they name: `expert_ids`: each token names two different experts. In each aligned block of 16 tokens (the tokens of one device) no expert is named by more than 6 tokens, a bound that some block reaches. `log_decay`: every entry is negative.
All inputs are finite; a program needn't handle non-finite values.
Results may differ from the reference program's by a relative error of at most 0.012.
Values may be sent and summed in bfloat16 or wider, within the bound.
No kernel may reach another device: no remote copies, remote signals or barrier semaphores. Data moves between devices by JAX's collectives and lax.ppermute only.
A program may use at most 128 MiB of HBM per device.

```python
import math
import jax
import jax.numpy as jnp
import numpy as np
from jax import lax

HEAD_TOTAL = 32
HD = 128
FF = 9216
BLOCK = 128
D = 4096
EXPERTS = 8
TOK_DEV = 16
CAP = 6
TOKEN_TOTAL = 4096
N_SEQ = 32


def draw_log_decay(key, part):
    key_collection = jax.random.split(jax.random.fold_in(key, 17), 6)
    slow_share = 0.5
    slow_heads = jax.random.uniform(key_collection[0], (HEAD_TOTAL,)) < slow_share
    slow_rate = jnp.exp(jax.random.uniform(key_collection[1], (HEAD_TOTAL,), minval=math.log(0.2), maxval=math.log(1.0))) / TOKEN_TOTAL
    fast_rate = jnp.exp(jax.random.uniform(key_collection[2], (HEAD_TOTAL,), minval=math.log(1.0 / 50.0), maxval=math.log(1.0 / 30.0)))
    baseline_decay_rate = jnp.where(slow_heads, slow_rate, fast_rate)
    multiplier = jnp.exp(jax.random.uniform(key_collection[3], (TOKEN_TOTAL, HEAD_TOTAL), minval=math.log(0.5), maxval=math.log(2.0)))
    spike_rows = jax.random.uniform(key_collection[4], (TOKEN_TOTAL, 1)) < 2.0 / TOKEN_TOTAL
    spike_loss = jnp.log(jax.random.uniform(key_collection[5], (TOKEN_TOTAL, HEAD_TOTAL), minval=0.5, maxval=0.8))
    final_output = -(baseline_decay_rate[None, :] * multiplier) + jnp.where(spike_rows, spike_loss, 0.0)
    return final_output.astype(jnp.float32)


def steps_of(key, shape, pieces, smallest, largest):
    def one(axis_at, blocks):
        steps = jax.random.uniform(jax.random.fold_in(jax.random.fold_in(key, 6), axis_at), (blocks,), jnp.float32, smallest / len(pieces), largest / len(pieces))
        return jnp.repeat(jnp.exp(steps), shape[axis_at] // blocks).reshape((-1,) + (1,) * (len(shape) - axis_at - 1))

    level = one(*pieces[0])
    for cut in pieces[1:]:
        level = level * one(*cut)
    return level


def deal_out(rng, own, number, rows, amount, top, most, slope):
    ranking = jax.random.permutation(rng, amount)
    packed, ordinary = shares(amount, rows * top, most, slope, True), shares(amount, rows * top, most, slope, False)
    places = jnp.arange(amount)

    def named(tallies, rotation):
        used = int((tallies > 0).sum())
        fixed = max(1, used // 4)
        shifted = fixed + (places - fixed + rotation * (used - fixed)) % max(1, amount - fixed)
        return jnp.zeros((amount,), jnp.int32).at[ranking[jnp.where(places < fixed, places, shifted)]].set(jnp.asarray(tallies, jnp.int32))

    tallies = jnp.where(number % 4 == 0, named(packed, number // 4), named(ordinary, number - number // 4 - 1))
    mixed = jax.random.permutation(jax.random.fold_in(own, 3), amount)
    source_of, taker = mixed[0:amount // 2 * 2:2], mixed[1:amount // 2 * 2:2]
    room = jnp.minimum(tallies[source_of] - 1, most - tallies[taker]) // 2
    room = jnp.where((source_of == ranking[0]) | (taker == ranking[0]) | (tallies[taker] == 0), 0, jnp.maximum(room, 0))
    shifted = jax.random.randint(jax.random.fold_in(own, 4), (amount // 2,), 0, 1 << 20) % (room + 1)
    tallies = tallies.at[source_of].add(-shifted).at[taker].add(shifted)
    members = jnp.searchsorted(jnp.cumsum(tallies), jnp.arange(rows * top), side="right").astype(jnp.int32)
    table = members.reshape(top, rows).T
    table = table[jax.random.permutation(jax.random.fold_in(own, 1), rows)]
    rotation = jax.random.randint(jax.random.fold_in(own, 2), (rows, 1), 0, top)
    return jnp.take_along_axis(table, (jnp.arange(top)[None, :] + rotation) % top, axis=1)


def shares(count, total, most, lean, full):
    weights = [(1 << 20) // math.isqrt(grade ** lean) + 1 for grade in range(1, count + 1)]
    largest = most if full else min(most, max(-(-total // count), total * weights[0] // sum(weights)))
    least = 1 if total - largest >= count - 1 else 0
    given, surplus = [largest] + [least] * (count - 1), total - largest - least * (count - 1)
    while surplus > 0:
        free = [i for i in range(1, count) if given[i] < largest] or [i for i in range(1, count) if given[i] < most]
        pool, remaining = sum([weights[i] for i in free]), surplus
        for i in free:
            more = min(most - given[i], max(1, remaining * weights[i] // pool), surplus)
            given[i] = given[i] + more
            surplus = surplus - more
    return np.array(given)


def noise(rng, dims, deviation, reach, pieces=(), kind=jnp.bfloat16):
    entries = jax.random.normal(rng, dims, jnp.float32) * deviation
    if len(pieces) > 0:
        entries = steps_of(rng, dims, pieces, -0.22, 0.18) * entries
    return jnp.clip(entries, min=-reach, max=reach).astype(kind)


def setup_inputs(seed: int = 0) -> dict:
    seeds = jax.random.split(jax.random.key(seed), 13)
    queries = noise(seeds[0], (TOKEN_TOTAL, D), 0.15, 2.0, ((0, 32), (1, 8)))
    keys = noise(seeds[1], (TOKEN_TOTAL, D), 0.15, 2.0, ((0, 32), (1, 8)))
    values = noise(seeds[2], (TOKEN_TOTAL, D), 1.0, 6.0, ((0, 32), (1, 8)))
    log_decay = draw_log_decay(jax.random.fold_in(seeds[12], 71), 0)
    residual = noise(seeds[4], (TOKEN_TOTAL, D), 1.0, 6.0, ((0, 256),))
    attn_gain = jnp.clip(1.0 + 0.15 * jax.random.normal(seeds[5], (D,), jnp.float32), 0.25, 1.75)
    moe_gain = jnp.clip(1.0 + 0.15 * jax.random.normal(seeds[6], (D,), jnp.float32), 0.25, 1.75)
    expert_ids_keys = jax.random.split(jax.random.fold_in(seeds[7], 1), TOKEN_TOTAL // TOK_DEV)
    expert_ids_turns = jax.random.permutation(jax.random.fold_in(seeds[7], 3), TOKEN_TOTAL // TOK_DEV)
    expert_ids = jax.vmap(lambda own, number: deal_out(jax.random.fold_in(seeds[7], 2), own, number, TOK_DEV, EXPERTS, 2, CAP, 2))(expert_ids_keys, expert_ids_turns).reshape((TOKEN_TOTAL, 2))
    gate_weights = jnp.clip(0.2 + 0.8 * jax.random.uniform(seeds[8], (TOKEN_TOTAL, 2), jnp.float32) ** steps_of(seeds[8], (TOKEN_TOTAL, 2), ((0, 256),), -0.2, 0.2), 0.2, 1.0)
    w_gate = noise(seeds[9], (EXPERTS, FF, D), D ** -0.5, 0.09375, ((0, 8), (1, 32)))
    w_up = noise(seeds[10], (EXPERTS, FF, D), D ** -0.5, 0.09375, ((0, 8), (1, 32)))
    w_down = noise(seeds[11], (EXPERTS, FF, D), FF ** -0.5, 0.0625, ((0, 8), (1, 32)))
    return {"queries": queries, "keys": keys, "values": values, "log_decay": log_decay, "residual": residual, "attn_gain": attn_gain, "moe_gain": moe_gain, "expert_ids": expert_ids, "gate_weights": gate_weights, "w_gate": w_gate, "w_up": w_up, "w_down": w_down}


def attend_block(state, inputs):
    q_blk, k_blk, v_blk, decay_blk = inputs
    rows = q_blk.shape[0]
    q_heads = q_blk.reshape(rows, HEAD_TOTAL, HD).astype(jnp.float32)
    k_heads = k_blk.reshape(rows, HEAD_TOTAL, HD).astype(jnp.float32)
    v_heads = v_blk.reshape(rows, HEAD_TOTAL, HD).astype(jnp.float32)
    log_cum = jnp.cumsum(decay_blk, axis=0)
    block_total = log_cum[-1]
    scores = jnp.einsum('thd,shd->hts', q_heads, k_heads)
    gap_logs = log_cum.T[:, :, None] - log_cum.T[:, None, :]
    causal_mask = (lax.broadcasted_iota(jnp.int32, (rows, rows), 0) >= lax.broadcasted_iota(jnp.int32, (rows, rows), 1))[None, :, :]
    weights = jnp.where(causal_mask, scores * jnp.exp(jnp.where(causal_mask, gap_logs, 0.0)), 0.0).astype(jnp.bfloat16)
    intra = jnp.einsum('hts,she->the', weights.astype(jnp.float32), v_heads)
    inter = jnp.exp(log_cum)[:, :, None] * jnp.einsum('thd,hde->the', q_heads, state, precision=lax.Precision.HIGHEST)
    attn = intra + inter
    keys_weighted = (k_heads * jnp.exp(block_total[None, :] - log_cum)[:, :, None]).astype(jnp.bfloat16)
    block_state = jnp.einsum('thd,the->hde', keys_weighted.astype(jnp.float32), v_heads)
    new_state = jnp.exp(block_total)[:, None, None] * state + block_state
    normed = (attn * lax.rsqrt(lax.optimization_barrier(jnp.mean(attn * attn, axis=-1, keepdims=True)) + 1e-06)).astype(jnp.bfloat16)
    return (new_state, normed.reshape(rows, HEAD_TOTAL * HD))

def route_targets(ids_block):
    flat_ids = ids_block.reshape(-1).astype(jnp.int32)
    onehot = (flat_ids[:, None] == jnp.arange(EXPERTS, dtype=jnp.int32)[None, :]).astype(jnp.int32)
    before = jnp.cumsum(onehot, axis=0) - onehot
    slot_index = lax.optimization_barrier(jnp.sum(before * onehot, axis=1)).astype(jnp.int32)
    return (flat_ids * CAP + slot_index).astype(jnp.int32)

def reference(queries, keys, values, log_decay, residual, attn_gain, moe_gain, expert_ids, gate_weights, w_gate, w_up, w_down):
    width = HEAD_TOTAL * HD
    blocks = TOKEN_TOTAL // BLOCK
    q_all = queries.reshape(blocks, BLOCK, width)
    k_all = keys.reshape(blocks, BLOCK, width)
    v_all = values.reshape(blocks, BLOCK, width)
    d_all = log_decay.reshape(blocks, BLOCK, HEAD_TOTAL)
    start_state = jnp.zeros((HEAD_TOTAL, HD, HD), jnp.float32)
    unused, normed = lax.scan(attend_block, start_state, (q_all, k_all, v_all, d_all))
    normed = normed.reshape(TOKEN_TOTAL, width)
    hidden = (residual.astype(jnp.float32) + normed.astype(jnp.float32) * attn_gain).astype(jnp.bfloat16)
    hid32 = hidden.astype(jnp.float32)
    moe_in = (hid32 * lax.rsqrt(lax.optimization_barrier(jnp.mean(hid32 * hid32, axis=-1, keepdims=True)) + 1e-06) * moe_gain).astype(jnp.bfloat16)
    groups = TOKEN_TOTAL // TOK_DEV
    moe_groups = moe_in.reshape(groups, TOK_DEV, width)
    ids_groups = expert_ids.reshape(groups, TOK_DEV * 2)
    targets = jax.vmap(route_targets)(ids_groups)

    def fill(moe_blk, target):
        doubled = jnp.repeat(moe_blk, 2, axis=0)
        return jnp.zeros((EXPERTS * CAP, width), jnp.bfloat16).at[target].set(doubled)
    buffers = jax.vmap(fill)(moe_groups, targets).reshape(groups, EXPERTS, CAP, width)
    slice_len = FF // N_SEQ

    def one_expert(index):
        rows_in = lax.dynamic_index_in_dim(buffers, index, 1, keepdims=False).reshape(groups * CAP, width).astype(jnp.float32)
        gate_mat = lax.dynamic_index_in_dim(w_gate, index, 0, keepdims=False).astype(jnp.float32)
        up_mat = lax.dynamic_index_in_dim(w_up, index, 0, keepdims=False).astype(jnp.float32)
        down_mat = lax.dynamic_index_in_dim(w_down, index, 0, keepdims=False).astype(jnp.float32)
        gate_part = jnp.dot(rows_in, gate_mat.T, preferred_element_type=jnp.float32, precision=lax.Precision.HIGHEST)
        up_part = jnp.dot(rows_in, up_mat.T, preferred_element_type=jnp.float32, precision=lax.Precision.HIGHEST)
        active = (jax.nn.silu(gate_part) * up_part).astype(jnp.bfloat16)
        active = lax.optimization_barrier(active).astype(jnp.float32)
        act_slices = active.reshape(groups * CAP, N_SEQ, slice_len).transpose(1, 0, 2)
        down_slices = down_mat.reshape(N_SEQ, slice_len, width)

        def add_slice(total, pair):
            part = jnp.dot(pair[0], pair[1], preferred_element_type=jnp.float32, precision=lax.Precision.HIGHEST).astype(jnp.bfloat16)
            return (total + part.astype(jnp.float32), None)
        total, unused_parts = lax.scan(add_slice, jnp.zeros((groups * CAP, width), jnp.float32), (act_slices, down_slices))
        return total.astype(jnp.bfloat16).reshape(groups, CAP, width)
    expert_out = lax.map(one_expert, jnp.arange(EXPERTS, dtype=jnp.int32))
    expert_out = expert_out.transpose(1, 0, 2, 3).reshape(groups, EXPERTS * CAP, width)

    def pick_rows(table, target):
        return table[target]
    picked = jax.vmap(pick_rows)(expert_out, targets).reshape(groups, TOK_DEV, 2, width)
    gates = gate_weights.reshape(groups, TOK_DEV, 2)
    mixed = hid32.reshape(groups, TOK_DEV, width) + lax.optimization_barrier(jnp.sum(gates[:, :, :, None] * picked.astype(jnp.float32), axis=2))
    return mixed.astype(jnp.bfloat16).reshape(TOKEN_TOTAL, width)
```

```python
import jax
import jax.numpy as jnp
from jax import lax
from jax.sharding import PartitionSpec as P

BF = jnp.bfloat16
F32 = jnp.float32
NX, NZ = 4, 8
CAP = 6


def shift_x(value, by):
    pairs = [(x * NZ + z, ((x + by) % NX) * NZ + z) for x in range(NX) for z in range(NZ)]
    return lax.ppermute(value, "seq", pairs)


def shift_z(value, by):
    pairs = [(x * NZ + z, x * NZ + (z + by) % NZ) for x in range(NX) for z in range(NZ)]
    return lax.ppermute(value, "seq", pairs)


def plus(a, b):
    return (a.astype(F32) + b.astype(F32)).astype(BF)


def plus_head(a, b):
    n = b.shape[0]
    return jnp.concatenate([plus(a[:n], b), a[n:]], axis=0)


def plus_tail(a, b):
    n = a.shape[0] - b.shape[0]
    return jnp.concatenate([a[:n], plus(a[n:], b)], axis=0)


def gather_z(own):
    half = own.shape[0] // 2
    r1, l1 = shift_z(own, 1), shift_z(own, -1)
    r2, l2 = shift_z(r1, 1), shift_z(l1, -1)
    r3, l3 = shift_z(r2, 1), shift_z(l2, -1)
    r4, l4 = shift_z(r3[:half], 1), shift_z(l3[half:], -1)
    return own, r1, l1, r2, l2, r3, l3, r4, l4


def reduce_z(pieces):
    own, r1, l1, r2, l2, r3, l3, r4, l4 = pieces
    a, b = shift_z(r4, -1), shift_z(l4, 1)
    a, b = shift_z(plus_head(r3, a), -1), shift_z(plus_tail(l3, b), 1)
    a, b = shift_z(plus(r2, a), -1), shift_z(plus(l2, b), 1)
    a, b = shift_z(plus(r1, a), -1), shift_z(plus(l1, b), 1)
    return own.astype(F32) + a.astype(F32) + b.astype(F32)


def gather_x(own):
    half = own.shape[0] // 2
    r1, l1 = shift_x(own, 1), shift_x(own, -1)
    r2, l2 = shift_x(r1[:half], 1), shift_x(l1[half:], -1)
    return own, r1, l1, r2, l2


def reduce_x(pieces):
    own, r1, l1, r2, l2 = pieces
    a, b = shift_x(r2, -1), shift_x(l2, 1)
    a, b = shift_x(plus_head(r1, a), -1), shift_x(plus_tail(l1, b), 1)
    return (own.astype(F32) + a.astype(F32) + b.astype(F32)).astype(BF)


def cut(value, sizes):
    out, at = [], 0
    for n in sizes:
        out.append(value[at : at + n])
        at += n
    return out


def parts_of_log(total):
    first = lax.reduce_precision(total, 8, 7)
    second = lax.reduce_precision(total - first, 8, 7)
    third = total - first - second
    return first.astype(BF), second.astype(BF), third.astype(BF)


def carried_state(block_total, block_state):
    heads = block_total.shape[0]
    seqs = lax.axis_size("seq")
    state = block_state.astype(BF).reshape(seqs, -1, 128)
    each = state.shape[1]
    marks = jnp.stack(parts_of_log(block_total), axis=0)
    marks = jnp.repeat(marks, seqs // heads, axis=1).T
    marks = jnp.broadcast_to(marks[:, :, None], (seqs, 3, 128))
    marks = jnp.concatenate([marks, jnp.zeros((seqs, 5, 128), BF)], axis=1)
    sent = jnp.concatenate([state, marks], axis=1)
    got = lax.all_to_all(sent, "seq", split_axis=0, concat_axis=0, tiled=True)
    totals = jnp.sum(got[:, each : each + 3, 0].astype(F32), axis=1)
    row = lax.broadcasted_iota(jnp.int32, (seqs, seqs), 0)
    col = lax.broadcasted_iota(jnp.int32, (seqs, seqs), 1)
    upto = jnp.sum(jnp.where(row >= col, totals[None, :], 0.0), axis=1)
    before = upto - totals
    gap = jnp.where(row > col, before[:, None] - upto[None, :], 0.0)
    weight = jnp.where(row > col, jnp.exp(gap), 0.0)
    states = got[:, :each, :].reshape(seqs, -1).astype(F32)
    summed = jnp.dot(weight, states, precision=lax.Precision.HIGHEST).astype(BF)
    back = lax.all_to_all(
        summed.reshape(seqs, each, 128), "seq", split_axis=0, concat_axis=0, tiled=True
    )
    return back.reshape(heads, 128, 128)


def route_targets(ids_block, experts):
    flat_ids = ids_block.reshape(-1)
    onehot = (flat_ids[:, None] == jnp.arange(experts, dtype=jnp.int32)[None, :]).astype(F32)
    n = flat_ids.shape[0]
    earlier = (jnp.arange(n)[:, None] > jnp.arange(n)[None, :]).astype(F32)
    before = jnp.dot(earlier, onehot, preferred_element_type=F32)
    slot = jnp.sum(before * onehot, axis=1).astype(jnp.int32)
    return flat_ids * CAP + slot


def body(
    queries,
    keys,
    values,
    log_decay,
    residual,
    attn_gain,
    moe_gain,
    expert_ids,
    gate_weights,
    w_gate,
    w_up,
    w_down,
):
    rows = queries.shape[0]
    heads = log_decay.shape[1]
    hd = queries.shape[1] // heads
    exps = lax.axis_size("exp")
    tok_rows, width = residual.shape
    share = width // exps
    place = lax.axis_index("exp")

    marked = jnp.concatenate(
        [residual, jnp.pad(expert_ids.astype(BF), ((0, 0), (0, 126)))], axis=1
    )
    block_tokens = lax.all_gather(marked, "exp", axis=0, tiled=True)
    res_cols = lax.dynamic_slice_in_dim(block_tokens, place * share, share, axis=1)
    block_ids = block_tokens[:, width : width + 2].astype(jnp.int32)
    gain_cols = lax.dynamic_slice_in_dim(attn_gain, place * share, share, axis=0)

    q_heads = queries.reshape(rows, heads, hd)
    k_heads = keys.reshape(rows, heads, hd)
    v_heads = values.reshape(rows, heads, hd)
    causal = lax.broadcasted_iota(jnp.int32, (rows, rows), 0) >= lax.broadcasted_iota(
        jnp.int32, (rows, rows), 1
    )
    log_cum = jnp.dot(causal.astype(F32), log_decay, precision=lax.Precision.HIGHEST)
    block_total = log_cum[-1]
    keys_weighted = (k_heads * jnp.exp(block_total[None, :] - log_cum)[:, :, None]).astype(BF)
    block_state = jnp.einsum("thd,the->hde", keys_weighted, v_heads, preferred_element_type=F32)
    carried = carried_state(block_total, block_state)
    scores = jnp.einsum("thd,shd->hts", q_heads, k_heads, preferred_element_type=F32)
    gap_logs = log_cum.T[:, :, None] - log_cum.T[:, None, :]
    mask = causal[None, :, :]
    weights = jnp.where(mask, scores * jnp.exp(jnp.where(mask, gap_logs, 0.0)), 0.0).astype(BF)
    intra = jnp.einsum("hts,she->the", weights, v_heads, preferred_element_type=F32)
    inter = jnp.exp(log_cum)[:, :, None] * jnp.einsum(
        "thd,hde->the", q_heads, carried, preferred_element_type=F32
    )
    attn = intra + inter
    normed = (attn * lax.rsqrt(jnp.mean(attn * attn, axis=-1, keepdims=True) + 1e-06)).astype(BF)
    normed = normed.reshape(rows, heads * hd)
    hidden_cols = (res_cols.astype(F32) + normed.astype(F32) * gain_cols[None, :]).astype(BF)

    slots = exps * CAP
    targets = jax.vmap(lambda ids: route_targets(ids, exps))(
        block_ids.reshape(exps, tok_rows, 2)
    ).reshape(exps, tok_rows, 2)
    slot_range = jnp.arange(slots, dtype=jnp.int32)
    hit = jnp.any(targets[:, None, :, :] == slot_range[None, :, None, None], axis=3)
    picker = hit.astype(BF)
    outgoing = jnp.einsum(
        "jkt,jtd->kjd",
        picker,
        hidden_cols.reshape(exps, tok_rows, share),
        preferred_element_type=F32,
    ).astype(BF)
    outgoing = outgoing.reshape(exps, CAP * exps, share)
    arrived = lax.all_to_all(outgoing, "exp", split_axis=0, concat_axis=0, tiled=True)
    hid_rows = arrived.transpose(1, 0, 2).reshape(slots, width)
    hid32_rows = hid_rows.astype(F32)
    moe_rows = (
        hid32_rows
        * lax.rsqrt(jnp.mean(hid32_rows * hid32_rows, axis=-1, keepdims=True) + 1e-06)
        * moe_gain
    ).astype(BF)

    hidden_all = lax.all_gather(hidden_cols, "exp", axis=0, tiled=False)
    hidden_own = lax.dynamic_slice_in_dim(hidden_all, place * tok_rows, tok_rows, axis=1)
    hidden_own = hidden_own.transpose(1, 0, 2).reshape(tok_rows, width)

    gate_w, up_w, down_w = w_gate[0], w_up[0], w_down[0]

    def ffn(x):
        gate_part = jnp.einsum("md,fd->mf", x, gate_w, preferred_element_type=F32)
        up_part = jnp.einsum("md,fd->mf", x, up_w, preferred_element_type=F32)
        active = (jax.nn.silu(gate_part) * up_part).astype(BF)
        return jnp.dot(active, down_w, preferred_element_type=F32).astype(BF)

    g1, g2 = moe_rows[:16], moe_rows[16:]
    a_r, a_l, a_2 = shift_x(g1, 1), shift_x(g1, -1), shift_x(g1, 2)
    own, r1, l1, r2, l2, r3, l3, r4, l4 = gather_z(g2)
    a_pieces = gather_z(jnp.concatenate([g1, a_r, a_l, a_2], axis=0))
    near = gather_x(jnp.concatenate([own, r1, l1], axis=0))
    far = gather_x(jnp.concatenate([r2, l2, r3, l3, r4, l4], axis=0))
    out_near = ffn(jnp.concatenate(near, axis=0))
    out_a = ffn(jnp.concatenate(a_pieces, axis=0))
    out_far = ffn(jnp.concatenate(far, axis=0))

    far_sum = reduce_x(cut(out_far, [p.shape[0] for p in far]))
    near_sum = reduce_x(cut(out_near, [p.shape[0] for p in near]))
    a_sum = reduce_z(cut(out_a, [p.shape[0] for p in a_pieces])).astype(BF)
    s_r2, s_l2, s_r3, s_l3, s_r4, s_l4 = cut(far_sum, (32, 32, 32, 32, 16, 16))
    s_own, s_r1, s_l1 = cut(near_sum, (32, 32, 32))
    g2_sum = reduce_z((s_own, s_r1, s_l1, s_r2, s_l2, s_r3, s_l3, s_r4, s_l4))
    b_own, b_r, b_l, b_2 = cut(a_sum, (16, 16, 16, 16))
    g1_sum = (
        b_own.astype(F32)
        + shift_x(b_r, -1).astype(F32)
        + shift_x(b_l, 1).astype(F32)
        + shift_x(b_2, 2).astype(F32)
    )
    expert_rows = jnp.concatenate([g1_sum, g2_sum], axis=0).astype(BF)

    by_block = expert_rows.reshape(CAP, exps, width).transpose(1, 0, 2)
    returned = lax.all_to_all(by_block, "exp", split_axis=0, concat_axis=0, tiled=True)
    flat_back = returned.reshape(slots, width)
    target = route_targets(expert_ids, exps).reshape(tok_rows, 2)
    chosen = (target[:, :, None] == slot_range[None, None, :]).astype(BF)
    picked = jnp.einsum("trk,kd->trd", chosen, flat_back, preferred_element_type=F32)
    mixed = hidden_own.astype(F32) + jnp.sum(gate_weights[:, :, None] * picked, axis=1)
    return mixed.astype(BF)


def solution(mesh):
    in_specs = (
        P("seq", "exp"),
        P("seq", "exp"),
        P("seq", "exp"),
        P("seq", "exp"),
        P(("seq", "exp"), None),
        P(),
        P(),
        P(("seq", "exp"), None),
        P(("seq", "exp"), None),
        P("exp", "seq", None),
        P("exp", "seq", None),
        P("exp", "seq", None),
    )
    out_specs = P(("seq", "exp"), None)
    return jax.shard_map(body, mesh=mesh, in_specs=in_specs, out_specs=out_specs, check_vma=False)
```

```python
import functools

import jax
import jax.numpy as jnp
from jax import lax
from jax.experimental import pallas as pl
from jax.experimental.pallas import tpu as pltpu
from jax.sharding import PartitionSpec as P

BF = jnp.bfloat16
F32 = jnp.float32
NX, NZ = 4, 8
CAP = 6


def shift_x(value, by):
    pairs = [(x * NZ + z, ((x + by) % NX) * NZ + z) for x in range(NX) for z in range(NZ)]
    return lax.ppermute(value, "seq", pairs)


def shift_z(value, by):
    pairs = [(x * NZ + z, x * NZ + (z + by) % NZ) for x in range(NX) for z in range(NZ)]
    return lax.ppermute(value, "seq", pairs)


def plus(a, b):
    return (a.astype(F32) + b.astype(F32)).astype(BF)


def plus_head(a, b):
    n = b.shape[0]
    return jnp.concatenate([plus(a[:n], b), a[n:]], axis=0)


def plus_tail(a, b):
    n = a.shape[0] - b.shape[0]
    return jnp.concatenate([a[:n], plus(a[n:], b)], axis=0)


def plus3(a, b, c):
    return (a.astype(F32) + b.astype(F32) + c.astype(F32)).astype(BF)


def cut(value, sizes):
    out, at = [], 0
    for n in sizes:
        out.append(value[at : at + n])
        at += n
    return out


def ffn_kernel(sources, sizes, *refs):
    n, given = len(sizes), max(which for which, _ in sources) + 1
    held, (gate_hbm, up_hbm, down_hbm) = refs[:given], refs[given : given + 3]
    outs = refs[given + 3 : given + 3 + n]
    x, gate, up, down, active, y, sem_x, sem_w, sem_y = refs[given + 3 + n :]
    pieces = [held[which].at[pl.ds(at, size)] for (which, at), size in zip(sources, sizes)]
    hidden, width = gate.shape
    main = hidden // 256 * 256
    starts = [sum(sizes[:i]) for i in range(n)]
    loads = [
        pltpu.make_async_copy(pieces[i], x.at[pl.ds(starts[i], sizes[i])], sem_x.at[i])
        for i in range(n)
    ]
    weights = [
        pltpu.make_async_copy(src, dst, sem_w.at[i])
        for i, (src, dst) in enumerate(((gate_hbm, gate), (up_hbm, up), (down_hbm, down)))
    ]
    for copy in loads + weights:
        copy.start()
    for copy in loads:
        copy.wait()

    def product(rows, block):
        return lax.dot_general(
            rows, block, (((1,), (1,)), ((), ())), preferred_element_type=F32
        )

    weights[0].wait()
    g = product(x[...], gate[:main, :])
    weights[1].wait()
    u = product(x[...], up[:main, :])
    active[:, :main] = (g / (1.0 + jnp.exp(-g)) * u).astype(BF)
    rest = product(x[...], jnp.concatenate([gate[main:, :], up[main:, :]], axis=0))
    g, u = rest[:, : hidden - main], rest[:, hidden - main :]
    active[:, main:] = (g / (1.0 + jnp.exp(-g)) * u).astype(BF)
    weights[2].wait()
    step = 512

    @pl.loop(0, width // step)
    def _(j):
        cols = pl.ds(pl.multiple_of(j * step, step), step)
        y[:, cols] = jnp.dot(active[...], down[:, cols], preferred_element_type=F32).astype(BF)

    stores = [
        pltpu.make_async_copy(y.at[pl.ds(starts[i], sizes[i])], outs[i], sem_y.at[i])
        for i in range(n)
    ]
    for copy in stores:
        copy.start()
    for copy in stores:
        copy.wait()


def ffn(pieces, gate, up, down):
    held, sources, sizes = [], [], []
    for piece in pieces:
        array, at, size = piece if isinstance(piece, tuple) else (piece, 0, piece.shape[0])
        if not any(array is other for other in held):
            held.append(array)
        sources.append(([array is other for other in held].index(True), at))
        sizes.append(size)
    total, n = sum(sizes), len(sizes)
    hidden, width = gate.shape
    moved = 2 * (2 * total * width + 3 * hidden * width)
    return pl.pallas_call(
        functools.partial(ffn_kernel, sources, sizes),
        out_shape=[jax.ShapeDtypeStruct((size, width), BF) for size in sizes],
        in_specs=[pl.BlockSpec(memory_space=pl.ANY)] * (len(held) + 3),
        out_specs=[pl.BlockSpec(memory_space=pl.ANY)] * n,
        scratch_shapes=[
            pltpu.VMEM((total, width), BF),
            pltpu.VMEM((hidden, width), BF),
            pltpu.VMEM((hidden, width), BF),
            pltpu.VMEM((hidden, width), BF),
            pltpu.VMEM((total, hidden), BF),
            pltpu.VMEM((total, width), BF),
            pltpu.SemaphoreType.DMA((n,)),
            pltpu.SemaphoreType.DMA((3,)),
            pltpu.SemaphoreType.DMA((n,)),
        ],
        compiler_params=pltpu.CompilerParams(vmem_limit_bytes=32 * 2**20),
        cost_estimate=pl.CostEstimate(
            flops=6 * total * width * hidden, bytes_accessed=moved, transcendentals=total * hidden
        ),
    )(*held, gate, up, down)


def cat(*pieces):
    return jnp.concatenate(pieces, axis=0)


def gather_compute_reduce(rows, gate, up, down):
    a, b = rows[:16], rows[16:]
    am, ap, a2 = shift_x(a, 1), shift_x(a, -1), shift_x(a, 2)
    b1m, b1p = shift_z(b, 1), shift_z(b, -1)
    a0 = cat(a, am, ap, a2)
    zm, zp = shift_z(cat(a0, b1m), 1), shift_z(cat(b1p, a0), -1)
    x1 = cat(b, b1m, b1p)
    x1m, x1p = shift_x(x1, 1), shift_x(x1, -1)
    z1m, z1p = zm, zp
    zm, zp = shift_z(z1m, 1), shift_z(z1p, -1)
    x2 = cat(z1m[64:], z1p[:32])
    x2m, x2p = shift_x(cat(x2, x1m[:48]), 1), shift_x(cat(x2, x1p[48:]), -1)
    out_1 = ffn(
        (a0, (z1m, 0, 64), (z1p, 32, 64), x1, x1m, x1p), gate, up, down
    )
    z2m, z2p = zm, zp
    zm, zp = shift_z(z2m[:80], 1), shift_z(z2p[16:], -1)
    x3 = cat(z2m[64:], z2p[:32])
    x3m, x3p = shift_x(cat(x3, x2m[:32]), 1), shift_x(cat(x3, x2p[32:64]), -1)
    out_2 = ffn(
        (
            (z2m, 0, 64),
            (z2p, 32, 64),
            x2,
            (x2m, 0, 64),
            (x2p, 0, 64),
            (x2m, 64, 48),
            (x2p, 64, 48),
        ),
        gate,
        up,
        down,
    )
    z3m, z3p = zm, zp
    z4m, z4p = shift_z(z3m[:32], 1), shift_z(z3p[48:], -1)
    x4 = cat(z3m[64:], z3p[:16])
    x4m, x4p = shift_x(cat(x4, x3m[:32]), 1), shift_x(cat(x4, x3p[32:64]), -1)
    out_3 = ffn(
        (
            (z3m, 0, 64),
            (z3p, 16, 64),
            x4,
            x3,
            (x3m, 0, 64),
            (x3p, 0, 64),
            (x3m, 64, 32),
            (x3p, 64, 32),
        ),
        gate,
        up,
        down,
    )
    x5m, x5p = shift_x(x4m[:16], 1), shift_x(x4p[16:32], -1)
    out_4 = ffn(
        (z4m, z4p, (x4m, 0, 32), (x4p, 0, 32), (x4m, 32, 32), (x4p, 32, 32)), gate, up, down
    )
    out_5 = ffn((x5m, x5p), gate, up, down)

    a0, a1m, a1p, x1, x1m, x1p = out_1
    a2m, a2p, x2, x2m, x2p, x1m2, x1p2 = out_2
    a3m, a3p, x4, x3, x3m, x3p, x2m2, x2p2 = out_3
    a4m, a4p, x4m, x4p, x3m2, x3p2 = out_4
    x4m2, x4p2 = out_5
    zm, zp = shift_z(a4m, -1), shift_z(a4p, 1)
    xm, xp = shift_x(x4m2, -1), shift_x(x4p2, 1)
    zm, zp = shift_z(plus_head(a3m, zm), -1), shift_z(plus_tail(a3p, zp), 1)
    xm, xp = (
        shift_x(cat(plus_head(x4m, xm), x3m2), -1),
        shift_x(cat(plus_tail(x4p, xp), x3p2), 1),
    )
    (c4m, h3m), (c4p, h3p) = cut(xm, (32, 32)), cut(xp, (32, 32))
    b4m, b4p = cut(plus3(x4, c4m, c4p), (16, 16))
    zm, zp = (
        shift_z(cat(plus(a2m, zm), b4m), -1),
        shift_z(cat(b4p, plus(a2p, zp)), 1),
    )
    xm, xp = (
        shift_x(cat(plus_head(x3m, h3m), x2m2), -1),
        shift_x(cat(plus_tail(x3p, h3p), x2p2), 1),
    )
    (c3m, h2m), (c3p, h2p) = cut(xm, (64, 32)), cut(xp, (64, 32))
    b3m, b3p = cut(plus3(x3, c3m, c3p), (32, 32))
    (zm, d4m), (d4p, zp) = cut(zm, (64, 16)), cut(zp, (16, 64))
    zm, zp = (
        shift_z(cat(plus(a1m, zm), plus_head(b3m, d4m)), -1),
        shift_z(cat(plus_tail(b3p, d4p), plus(a1p, zp)), 1),
    )
    xm, xp = (
        shift_x(cat(plus_head(x2m, h2m), x1m2), -1),
        shift_x(cat(plus_tail(x2p, h2p), x1p2), 1),
    )
    (c2m, h1m), (c2p, h1p) = cut(xm, (64, 48)), cut(xp, (64, 48))
    b2m, b2p = cut(plus3(x2, c2m, c2p), (32, 32))
    (zm, d3m), (d3p, zp) = cut(zm, (64, 32)), cut(zp, (32, 64))
    a, am, ap, a2 = cut(plus3(a0, zm, zp), (16, 16, 16, 16))
    d2m, d2p = shift_z(plus(b2m, d3m), -1), shift_z(plus(b2p, d3p), 1)
    xm, xp = (
        shift_x(cat(plus_head(x1m, h1m), am), -1),
        shift_x(cat(plus_tail(x1p, h1p), ap), 1),
    )
    a2 = shift_x(a2, 2)
    (c1m, am), (c1p, ap) = cut(xm, (96, 16)), cut(xp, (96, 16))
    b, b1m, b1p = cut(plus3(x1, c1m, c1p), (32, 32, 32))
    d1m, d1p = shift_z(plus(b1m, d2m), -1), shift_z(plus(b1p, d2p), 1)
    a_sum = a.astype(F32) + am.astype(F32) + ap.astype(F32) + a2.astype(F32)
    b_sum = b.astype(F32) + d1m.astype(F32) + d1p.astype(F32)
    return a_sum, b_sum


def parts_of_log(total):
    first = lax.reduce_precision(total, 8, 7)
    second = lax.reduce_precision(total - first, 8, 7)
    third = total - first - second
    return first.astype(BF), second.astype(BF), third.astype(BF)


def carried_state(block_total, block_state):
    heads = block_total.shape[0]
    seqs = lax.axis_size("seq")
    state = block_state.astype(BF).reshape(seqs, -1, 128)
    each = state.shape[1]
    marks = jnp.stack(parts_of_log(block_total), axis=0)
    marks = jnp.repeat(marks, seqs // heads, axis=1).T
    marks = jnp.broadcast_to(marks[:, :, None], (seqs, 3, 128))
    marks = jnp.concatenate([marks, jnp.zeros((seqs, 5, 128), BF)], axis=1)
    sent = jnp.concatenate([state, marks], axis=1)
    got = lax.all_to_all(sent, "seq", split_axis=0, concat_axis=0, tiled=True)
    totals = jnp.sum(got[:, each : each + 3, 0].astype(F32), axis=1)
    row = lax.broadcasted_iota(jnp.int32, (seqs, seqs), 0)
    col = lax.broadcasted_iota(jnp.int32, (seqs, seqs), 1)
    upto = jnp.sum(jnp.where(row >= col, totals[None, :], 0.0), axis=1)
    before = upto - totals
    gap = jnp.where(row > col, before[:, None] - upto[None, :], 0.0)
    weight = jnp.where(row > col, jnp.exp(gap), 0.0)
    states = got[:, :each, :].reshape(seqs, -1).astype(F32)
    summed = jnp.dot(weight, states, precision=lax.Precision.HIGHEST).astype(BF)
    back = lax.all_to_all(
        summed.reshape(seqs, each, 128), "seq", split_axis=0, concat_axis=0, tiled=True
    )
    return back.reshape(heads, 128, 128)


def route_targets(ids_block, experts):
    flat_ids = ids_block.reshape(-1)
    onehot = (flat_ids[:, None] == jnp.arange(experts, dtype=jnp.int32)[None, :]).astype(F32)
    n = flat_ids.shape[0]
    earlier = (jnp.arange(n)[:, None] > jnp.arange(n)[None, :]).astype(F32)
    before = jnp.dot(earlier, onehot, preferred_element_type=F32)
    slot = jnp.sum(before * onehot, axis=1).astype(jnp.int32)
    return flat_ids * CAP + slot


def body(
    queries,
    keys,
    values,
    log_decay,
    residual,
    attn_gain,
    moe_gain,
    expert_ids,
    gate_weights,
    w_gate,
    w_up,
    w_down,
):
    rows = queries.shape[0]
    heads = log_decay.shape[1]
    hd = queries.shape[1] // heads
    exps = lax.axis_size("exp")
    tok_rows, width = residual.shape
    share = width // exps
    place = lax.axis_index("exp")

    marked = jnp.concatenate(
        [residual, jnp.pad(expert_ids.astype(BF), ((0, 0), (0, 126)))], axis=1
    )
    block_tokens = lax.all_gather(marked, "exp", axis=0, tiled=True)
    res_cols = lax.dynamic_slice_in_dim(block_tokens, place * share, share, axis=1)
    block_ids = block_tokens[:, width : width + 2].astype(jnp.int32)
    gain_cols = lax.dynamic_slice_in_dim(attn_gain, place * share, share, axis=0)

    q_heads = queries.reshape(rows, heads, hd)
    k_heads = keys.reshape(rows, heads, hd)
    v_heads = values.reshape(rows, heads, hd)
    causal = lax.broadcasted_iota(jnp.int32, (rows, rows), 0) >= lax.broadcasted_iota(
        jnp.int32, (rows, rows), 1
    )
    log_cum = jnp.dot(causal.astype(F32), log_decay, precision=lax.Precision.HIGHEST)
    block_total = log_cum[-1]
    keys_weighted = (k_heads * jnp.exp(block_total[None, :] - log_cum)[:, :, None]).astype(BF)
    block_state = jnp.einsum("thd,the->hde", keys_weighted, v_heads, preferred_element_type=F32)
    carried = carried_state(block_total, block_state)
    scores = jnp.einsum("thd,shd->hts", q_heads, k_heads, preferred_element_type=F32)
    gap_logs = log_cum.T[:, :, None] - log_cum.T[:, None, :]
    mask = causal[None, :, :]
    weights = jnp.where(mask, scores * jnp.exp(jnp.where(mask, gap_logs, 0.0)), 0.0).astype(BF)
    intra = jnp.einsum("hts,she->the", weights, v_heads, preferred_element_type=F32)
    inter = jnp.exp(log_cum)[:, :, None] * jnp.einsum(
        "thd,hde->the", q_heads, carried, preferred_element_type=F32
    )
    attn = intra + inter
    normed = (attn * lax.rsqrt(jnp.mean(attn * attn, axis=-1, keepdims=True) + 1e-06)).astype(BF)
    normed = normed.reshape(rows, heads * hd)
    hidden_cols = (res_cols.astype(F32) + normed.astype(F32) * gain_cols[None, :]).astype(BF)

    slots = exps * CAP
    targets = jax.vmap(lambda ids: route_targets(ids, exps))(
        block_ids.reshape(exps, tok_rows, 2)
    ).reshape(exps, tok_rows, 2)
    slot_range = jnp.arange(slots, dtype=jnp.int32)
    hit = jnp.any(targets[:, None, :, :] == slot_range[None, :, None, None], axis=3)
    picker = hit.astype(BF)
    outgoing = jnp.einsum(
        "jkt,jtd->kjd",
        picker,
        hidden_cols.reshape(exps, tok_rows, share),
        preferred_element_type=F32,
    ).astype(BF)
    outgoing = outgoing.reshape(exps, CAP * exps, share)
    arrived = lax.all_to_all(outgoing, "exp", split_axis=0, concat_axis=0, tiled=True)
    hid_rows = arrived.transpose(1, 0, 2).reshape(slots, width)
    hid32_rows = hid_rows.astype(F32)
    moe_rows = (
        hid32_rows
        * lax.rsqrt(jnp.mean(hid32_rows * hid32_rows, axis=-1, keepdims=True) + 1e-06)
        * moe_gain
    ).astype(BF)

    hidden_all = lax.all_gather(hidden_cols, "exp", axis=0, tiled=False)
    hidden_own = lax.dynamic_slice_in_dim(hidden_all, place * tok_rows, tok_rows, axis=1)
    hidden_own = hidden_own.transpose(1, 0, 2).reshape(tok_rows, width)

    expert_sums = gather_compute_reduce(moe_rows, w_gate[0], w_up[0], w_down[0])
    expert_rows = jnp.concatenate(expert_sums, axis=0).astype(BF)

    by_block = expert_rows.reshape(CAP, exps, width).transpose(1, 0, 2)
    returned = lax.all_to_all(by_block, "exp", split_axis=0, concat_axis=0, tiled=True)
    flat_back = returned.reshape(slots, width)
    target = route_targets(expert_ids, exps).reshape(tok_rows, 2)
    chosen = (target[:, :, None] == slot_range[None, None, :]).astype(BF)
    picked = jnp.einsum("trk,kd->trd", chosen, flat_back, preferred_element_type=F32)
    mixed = hidden_own.astype(F32) + jnp.sum(gate_weights[:, :, None] * picked, axis=1)
    return mixed.astype(BF)


def solution(mesh):
    in_specs = (
        P("seq", "exp"),
        P("seq", "exp"),
        P("seq", "exp"),
        P("seq", "exp"),
        P(("seq", "exp"), None),
        P(),
        P(),
        P(("seq", "exp"), None),
        P(("seq", "exp"), None),
        P("exp", "seq", None),
        P("exp", "seq", None),
        P("exp", "seq", None),
    )
    out_specs = P(("seq", "exp"), None)
    return jax.shard_map(body, mesh=mesh, in_specs=in_specs, out_specs=out_specs, check_vma=False)
```

```python
import functools

import jax
import jax.numpy as jnp
from jax import lax
from jax.experimental import pallas as pl
from jax.experimental.pallas import tpu as pltpu
from jax.sharding import PartitionSpec as P

BF = jnp.bfloat16
F32 = jnp.float32
NX, NZ = 4, 8
CAP = 6


def shift_x(value, by):
    pairs = [(x * NZ + z, ((x + by) % NX) * NZ + z) for x in range(NX) for z in range(NZ)]
    return lax.ppermute(value, "seq", pairs)


def shift_z(value, by):
    pairs = [(x * NZ + z, x * NZ + (z + by) % NZ) for x in range(NX) for z in range(NZ)]
    return lax.ppermute(value, "seq", pairs)


def plus(a, b):
    return (a.astype(F32) + b.astype(F32)).astype(BF)


def plus_head(a, b):
    n = b.shape[0]
    return jnp.concatenate([plus(a[:n], b), a[n:]], axis=0)


def plus_tail(a, b):
    n = a.shape[0] - b.shape[0]
    return jnp.concatenate([a[:n], plus(a[n:], b)], axis=0)


def plus3(a, b, c):
    return (a.astype(F32) + b.astype(F32) + c.astype(F32)).astype(BF)


def cut(value, sizes):
    out, at = [], 0
    for n in sizes:
        out.append(value[at : at + n])
        at += n
    return out


def ffn_kernel(sources, sizes, *refs):
    n, given = len(sizes), max(which for which, _ in sources) + 1
    held, (gate, up, down) = refs[:given], refs[given : given + 3]
    outs = refs[given + 3 : given + 3 + n]
    x, active, y, sem_x, sem_y = refs[given + 3 + n :]
    pieces = [held[which].at[pl.ds(at, size)] for (which, at), size in zip(sources, sizes)]
    hidden, width = gate.shape
    main = hidden // 256 * 256
    starts = [sum(sizes[:i]) for i in range(n)]
    loads = [
        pltpu.make_async_copy(pieces[i], x.at[pl.ds(starts[i], sizes[i])], sem_x.at[i])
        for i in range(n)
    ]
    for copy in loads:
        copy.start()
    for copy in loads:
        copy.wait()

    def product(rows, block):
        return lax.dot_general(
            rows, block, (((1,), (1,)), ((), ())), preferred_element_type=F32
        )

    g = product(x[...], gate[:main, :])
    u = product(x[...], up[:main, :])
    active[:, :main] = (g / (1.0 + jnp.exp(-g)) * u).astype(BF)
    rest = product(x[...], jnp.concatenate([gate[main:, :], up[main:, :]], axis=0))
    g, u = rest[:, : hidden - main], rest[:, hidden - main :]
    active[:, main:] = (g / (1.0 + jnp.exp(-g)) * u).astype(BF)
    step = 512

    @pl.loop(0, width // step)
    def _(j):
        cols = pl.ds(pl.multiple_of(j * step, step), step)
        y[:, cols] = jnp.dot(active[...], down[:, cols], preferred_element_type=F32).astype(BF)

    stores = [
        pltpu.make_async_copy(y.at[pl.ds(starts[i], sizes[i])], outs[i], sem_y.at[i])
        for i in range(n)
    ]
    for copy in stores:
        copy.start()
    for copy in stores:
        copy.wait()


def ffn(pieces, gate, up, down):
    held, sources, sizes = [], [], []
    for piece in pieces:
        array, at, size = piece if isinstance(piece, tuple) else (piece, 0, piece.shape[0])
        if not any(array is other for other in held):
            held.append(array)
        sources.append(([array is other for other in held].index(True), at))
        sizes.append(size)
    total, n = sum(sizes), len(sizes)
    hidden, width = gate.shape
    moved = 2 * (2 * total * width + 3 * hidden * width)
    return pl.pallas_call(
        functools.partial(ffn_kernel, sources, sizes),
        out_shape=[jax.ShapeDtypeStruct((size, width), BF) for size in sizes],
        in_specs=[pl.BlockSpec(memory_space=pl.ANY)] * len(held)
        + [pl.BlockSpec(memory_space=pltpu.VMEM)] * 3,
        out_specs=[pl.BlockSpec(memory_space=pl.ANY)] * n,
        scratch_shapes=[
            pltpu.VMEM((total, width), BF),
            pltpu.VMEM((total, hidden), BF),
            pltpu.VMEM((total, width), BF),
            pltpu.SemaphoreType.DMA((n,)),
            pltpu.SemaphoreType.DMA((n,)),
        ],
        compiler_params=pltpu.CompilerParams(vmem_limit_bytes=32 * 2**20),
        cost_estimate=pl.CostEstimate(
            flops=6 * total * width * hidden, bytes_accessed=moved, transcendentals=total * hidden
        ),
    )(*held, gate, up, down)


def cat(*pieces):
    return jnp.concatenate(pieces, axis=0)


def gather_compute_reduce(rows, gate, up, down):
    a, b = rows[:16], rows[16:]
    am, ap, a2 = shift_x(a, 1), shift_x(a, -1), shift_x(a, 2)
    b1m, b1p = shift_z(b, 1), shift_z(b, -1)
    am, ap, a2, b1m, b1p = lax.optimization_barrier((am, ap, a2, b1m, b1p))
    a0 = cat(a, am, ap, a2)
    zm, zp = shift_z(cat(a0, b1m), 1), shift_z(cat(b1p, a0), -1)
    x1 = cat(b, b1m, b1p)
    x1m, x1p = shift_x(x1, 1), shift_x(x1, -1)
    z1m, z1p = zm, zp
    zm, zp = shift_z(z1m, 1), shift_z(z1p, -1)
    x2 = cat(z1m[64:], z1p[:32])
    x2m, x2p = shift_x(cat(x2, x1m[:48]), 1), shift_x(cat(x2, x1p[48:]), -1)
    out_1 = ffn(
        (a0, (z1m, 0, 64), (z1p, 32, 64), x1, x1m, x1p), gate, up, down
    )
    z2m, z2p = zm, zp
    z2m, z2p, x2m, x2p, out_1 = lax.optimization_barrier((z2m, z2p, x2m, x2p, out_1))
    zm, zp = shift_z(z2m[:80], 1), shift_z(z2p[16:], -1)
    x3 = cat(z2m[64:], z2p[:32])
    x3m, x3p = shift_x(cat(x3, x2m[:32]), 1), shift_x(cat(x3, x2p[32:64]), -1)
    out_2 = ffn(
        (
            (z2m, 0, 64),
            (z2p, 32, 64),
            x2,
            (x2m, 0, 64),
            (x2p, 0, 64),
            (x2m, 64, 48),
            (x2p, 64, 48),
        ),
        gate,
        up,
        down,
    )
    z3m, z3p = zm, zp
    z3m, z3p, x3m, x3p, out_2 = lax.optimization_barrier((z3m, z3p, x3m, x3p, out_2))
    z4m, z4p = shift_z(z3m[:32], 1), shift_z(z3p[48:], -1)
    x4 = cat(z3m[64:], z3p[:16])
    x4m, x4p = shift_x(cat(x4, x3m[:32]), 1), shift_x(cat(x4, x3p[32:64]), -1)
    out_3 = ffn(
        (
            (z3m, 0, 64),
            (z3p, 16, 64),
            x4,
            x3,
            (x3m, 0, 64),
            (x3p, 0, 64),
            (x3m, 64, 32),
            (x3p, 64, 32),
        ),
        gate,
        up,
        down,
    )
    z4m, z4p, x4m, x4p, out_3 = lax.optimization_barrier((z4m, z4p, x4m, x4p, out_3))
    x5m, x5p = shift_x(x4m[:16], 1), shift_x(x4p[16:32], -1)
    out_4 = ffn(
        (z4m, z4p, (x4m, 0, 32), (x4p, 0, 32), (x4m, 32, 32), (x4p, 32, 32)), gate, up, down
    )
    x5m, x5p, out_4 = lax.optimization_barrier((x5m, x5p, out_4))
    out_5 = ffn((x5m, x5p), gate, up, down)

    a0, a1m, a1p, x1, x1m, x1p = out_1
    a2m, a2p, x2, x2m, x2p, x1m2, x1p2 = out_2
    a3m, a3p, x4, x3, x3m, x3p, x2m2, x2p2 = out_3
    a4m, a4p, x4m, x4p, x3m2, x3p2 = out_4
    x4m2, x4p2 = out_5
    zm, zp = shift_z(a4m, -1), shift_z(a4p, 1)
    xm, xp = shift_x(x4m2, -1), shift_x(x4p2, 1)
    zm, zp = shift_z(plus_head(a3m, zm), -1), shift_z(plus_tail(a3p, zp), 1)
    xm, xp = (
        shift_x(cat(plus_head(x4m, xm), x3m2), -1),
        shift_x(cat(plus_tail(x4p, xp), x3p2), 1),
    )
    (c4m, h3m), (c4p, h3p) = cut(xm, (32, 32)), cut(xp, (32, 32))
    b4m, b4p = cut(plus3(x4, c4m, c4p), (16, 16))
    zm, zp = (
        shift_z(cat(plus(a2m, zm), b4m), -1),
        shift_z(cat(b4p, plus(a2p, zp)), 1),
    )
    xm, xp = (
        shift_x(cat(plus_head(x3m, h3m), x2m2), -1),
        shift_x(cat(plus_tail(x3p, h3p), x2p2), 1),
    )
    (c3m, h2m), (c3p, h2p) = cut(xm, (64, 32)), cut(xp, (64, 32))
    b3m, b3p = cut(plus3(x3, c3m, c3p), (32, 32))
    (zm, d4m), (d4p, zp) = cut(zm, (64, 16)), cut(zp, (16, 64))
    zm, zp = (
        shift_z(cat(plus(a1m, zm), plus_head(b3m, d4m)), -1),
        shift_z(cat(plus_tail(b3p, d4p), plus(a1p, zp)), 1),
    )
    xm, xp = (
        shift_x(cat(plus_head(x2m, h2m), x1m2), -1),
        shift_x(cat(plus_tail(x2p, h2p), x1p2), 1),
    )
    (c2m, h1m), (c2p, h1p) = cut(xm, (64, 48)), cut(xp, (64, 48))
    b2m, b2p = cut(plus3(x2, c2m, c2p), (32, 32))
    (zm, d3m), (d3p, zp) = cut(zm, (64, 32)), cut(zp, (32, 64))
    a, am, ap, a2 = cut(plus3(a0, zm, zp), (16, 16, 16, 16))
    d2m, d2p = shift_z(plus(b2m, d3m), -1), shift_z(plus(b2p, d3p), 1)
    xm, xp = (
        shift_x(cat(plus_head(x1m, h1m), am), -1),
        shift_x(cat(plus_tail(x1p, h1p), ap), 1),
    )
    a2 = shift_x(a2, 2)
    (c1m, am), (c1p, ap) = cut(xm, (96, 16)), cut(xp, (96, 16))
    b, b1m, b1p = cut(plus3(x1, c1m, c1p), (32, 32, 32))
    d1m, d1p = shift_z(plus(b1m, d2m), -1), shift_z(plus(b1p, d2p), 1)
    a_sum = a.astype(F32) + am.astype(F32) + ap.astype(F32) + a2.astype(F32)
    b_sum = b.astype(F32) + d1m.astype(F32) + d1p.astype(F32)
    return a_sum, b_sum


def parts_of_log(total):
    first = lax.reduce_precision(total, 8, 7)
    second = lax.reduce_precision(total - first, 8, 7)
    third = total - first - second
    return first.astype(BF), second.astype(BF), third.astype(BF)


def carried_state(block_total, block_state):
    heads = block_total.shape[0]
    seqs = lax.axis_size("seq")
    state = block_state.astype(BF).reshape(seqs, -1, 128)
    each = state.shape[1]
    marks = jnp.stack(parts_of_log(block_total), axis=0)
    marks = jnp.repeat(marks, seqs // heads, axis=1).T
    marks = jnp.broadcast_to(marks[:, :, None], (seqs, 3, 128))
    marks = jnp.concatenate([marks, jnp.zeros((seqs, 5, 128), BF)], axis=1)
    sent = jnp.concatenate([state, marks], axis=1)
    got = lax.all_to_all(sent, "seq", split_axis=0, concat_axis=0, tiled=True)
    totals = jnp.sum(got[:, each : each + 3, 0].astype(F32), axis=1)
    row = lax.broadcasted_iota(jnp.int32, (seqs, seqs), 0)
    col = lax.broadcasted_iota(jnp.int32, (seqs, seqs), 1)
    upto = jnp.sum(jnp.where(row >= col, totals[None, :], 0.0), axis=1)
    before = upto - totals
    gap = jnp.where(row > col, before[:, None] - upto[None, :], 0.0)
    weight = jnp.where(row > col, jnp.exp(gap), 0.0)
    states = got[:, :each, :].reshape(seqs, -1).astype(F32)
    summed = jnp.dot(weight, states, precision=lax.Precision.HIGHEST).astype(BF)
    back = lax.all_to_all(
        summed.reshape(seqs, each, 128), "seq", split_axis=0, concat_axis=0, tiled=True
    )
    return back.reshape(heads, 128, 128)


def route_targets(ids_block, experts):
    flat_ids = ids_block.reshape(-1)
    onehot = (flat_ids[:, None] == jnp.arange(experts, dtype=jnp.int32)[None, :]).astype(F32)
    n = flat_ids.shape[0]
    earlier = (jnp.arange(n)[:, None] > jnp.arange(n)[None, :]).astype(F32)
    before = jnp.dot(earlier, onehot, preferred_element_type=F32)
    slot = jnp.sum(before * onehot, axis=1).astype(jnp.int32)
    return flat_ids * CAP + slot


def body(
    queries,
    keys,
    values,
    log_decay,
    residual,
    attn_gain,
    moe_gain,
    expert_ids,
    gate_weights,
    w_gate,
    w_up,
    w_down,
):
    rows = queries.shape[0]
    heads = log_decay.shape[1]
    hd = queries.shape[1] // heads
    exps = lax.axis_size("exp")
    tok_rows, width = residual.shape
    share = width // exps
    place = lax.axis_index("exp")

    slots = exps * CAP
    target = route_targets(expert_ids, exps).reshape(tok_rows, 2)
    marked = jnp.concatenate(
        [residual, jnp.pad(target.astype(BF), ((0, 0), (0, 126)))], axis=1
    )
    block_tokens = lax.all_gather(marked, "exp", axis=0, tiled=True)
    res_cols = lax.dynamic_slice_in_dim(block_tokens, place * share, share, axis=1)
    targets = block_tokens[:, width : width + 2].astype(jnp.int32).reshape(exps, tok_rows, 2)
    gain_cols = lax.dynamic_slice_in_dim(attn_gain, place * share, share, axis=0)

    q_heads = queries.reshape(rows, heads, hd)
    k_heads = keys.reshape(rows, heads, hd)
    v_heads = values.reshape(rows, heads, hd)
    causal = lax.broadcasted_iota(jnp.int32, (rows, rows), 0) >= lax.broadcasted_iota(
        jnp.int32, (rows, rows), 1
    )
    log_cum = jnp.dot(causal.astype(F32), log_decay, precision=lax.Precision.HIGHEST)
    block_total = log_cum[-1]
    keys_weighted = (k_heads * jnp.exp(block_total[None, :] - log_cum)[:, :, None]).astype(BF)
    block_state = jnp.einsum("thd,the->hde", keys_weighted, v_heads, preferred_element_type=F32)
    carried = carried_state(block_total, block_state)
    scores = jnp.einsum("thd,shd->hts", q_heads, k_heads, preferred_element_type=F32)
    gap_logs = log_cum.T[:, :, None] - log_cum.T[:, None, :]
    mask = causal[None, :, :]
    weights = jnp.where(mask, scores * jnp.exp(jnp.where(mask, gap_logs, 0.0)), 0.0).astype(BF)
    intra = jnp.einsum("hts,she->the", weights, v_heads, preferred_element_type=F32)
    inter = jnp.exp(log_cum)[:, :, None] * jnp.einsum(
        "thd,hde->the", q_heads, carried, preferred_element_type=F32
    )
    attn = intra + inter
    normed = (attn * lax.rsqrt(jnp.mean(attn * attn, axis=-1, keepdims=True) + 1e-06)).astype(BF)
    normed = normed.reshape(rows, heads * hd)
    hidden_cols = (res_cols.astype(F32) + normed.astype(F32) * gain_cols[None, :]).astype(BF)

    slot_range = jnp.arange(slots, dtype=jnp.int32)
    hit = jnp.any(targets[:, None, :, :] == slot_range[None, :, None, None], axis=3)
    picker = hit.astype(BF)
    outgoing = jnp.einsum(
        "jkt,jtd->kjd",
        picker,
        hidden_cols.reshape(exps, tok_rows, share),
        preferred_element_type=F32,
    ).astype(BF)
    outgoing = outgoing.reshape(exps, CAP * exps, share)
    arrived = lax.all_to_all(outgoing, "exp", split_axis=0, concat_axis=0, tiled=True)
    hid_rows = arrived.transpose(1, 0, 2).reshape(slots, width)
    hid32_rows = hid_rows.astype(F32)
    moe_rows = (
        hid32_rows
        * lax.rsqrt(jnp.mean(hid32_rows * hid32_rows, axis=-1, keepdims=True) + 1e-06)
        * moe_gain
    ).astype(BF)

    hidden_all = lax.all_gather(hidden_cols, "exp", axis=0, tiled=False)
    hidden_own = lax.dynamic_slice_in_dim(hidden_all, place * tok_rows, tok_rows, axis=1)
    hidden_own = hidden_own.transpose(1, 0, 2).reshape(tok_rows, width)

    expert_sums = gather_compute_reduce(moe_rows, w_gate[0], w_up[0], w_down[0])
    expert_rows = jnp.concatenate(expert_sums, axis=0).astype(BF)

    by_block = expert_rows.reshape(CAP, exps, width).transpose(1, 0, 2)
    returned = lax.all_to_all(by_block, "exp", split_axis=0, concat_axis=0, tiled=True)
    flat_back = returned.reshape(slots, width)
    chosen = (target[:, :, None] == slot_range[None, None, :]).astype(BF)
    picked = jnp.einsum("trk,kd->trd", chosen, flat_back, preferred_element_type=F32)
    mixed = hidden_own.astype(F32) + jnp.sum(gate_weights[:, :, None] * picked, axis=1)
    return mixed.astype(BF)


def solution(mesh):
    in_specs = (
        P("seq", "exp"),
        P("seq", "exp"),
        P("seq", "exp"),
        P("seq", "exp"),
        P(("seq", "exp"), None),
        P(),
        P(),
        P(("seq", "exp"), None),
        P(("seq", "exp"), None),
        P("exp", "seq", None),
        P("exp", "seq", None),
        P("exp", "seq", None),
    )
    out_specs = P(("seq", "exp"), None)
    return jax.shard_map(body, mesh=mesh, in_specs=in_specs, out_specs=out_specs, check_vma=False)
```

```python
import functools

import jax
import jax.numpy as jnp
from jax import lax
from jax.experimental import pallas as pl
from jax.experimental.pallas import tpu as pltpu
from jax.sharding import PartitionSpec as P

BF = jnp.bfloat16
F32 = jnp.float32
NX, NZ = 4, 8
CAP = 6


def shift_x(value, by):
    pairs = [(x * NZ + z, ((x + by) % NX) * NZ + z) for x in range(NX) for z in range(NZ)]
    return lax.ppermute(value, "seq", pairs)


def shift_z(value, by):
    pairs = [(x * NZ + z, x * NZ + (z + by) % NZ) for x in range(NX) for z in range(NZ)]
    return lax.ppermute(value, "seq", pairs)


def plus(a, b):
    return (a.astype(F32) + b.astype(F32)).astype(BF)


def plus_head(a, b):
    n = b.shape[0]
    return jnp.concatenate([plus(a[:n], b), a[n:]], axis=0)


def plus_tail(a, b):
    n = a.shape[0] - b.shape[0]
    return jnp.concatenate([a[:n], plus(a[n:], b)], axis=0)


def plus3(a, b, c):
    return (a.astype(F32) + b.astype(F32) + c.astype(F32)).astype(BF)


def cut(value, sizes):
    out, at = [], 0
    for n in sizes:
        out.append(value[at : at + n])
        at += n
    return out


def ffn_kernel(sources, sizes, *refs):
    n, given = len(sizes), max(which for which, _ in sources) + 1
    held, (gate, up, down) = refs[:given], refs[given : given + 3]
    outs = refs[given + 3 : given + 3 + n]
    x, active, y, sem_x, sem_y = refs[given + 3 + n :]
    pieces = [held[which].at[pl.ds(at, size)] for (which, at), size in zip(sources, sizes)]
    hidden, width = gate.shape
    main = hidden // 256 * 256
    starts = [sum(sizes[:i]) for i in range(n)]
    loads = [
        pltpu.make_async_copy(pieces[i], x.at[pl.ds(starts[i], sizes[i])], sem_x.at[i])
        for i in range(n)
    ]
    for copy in loads:
        copy.start()
    for copy in loads:
        copy.wait()

    def product(rows, block):
        return lax.dot_general(
            rows, block, (((1,), (1,)), ((), ())), preferred_element_type=F32
        )

    g = product(x[...], gate[:main, :])
    u = product(x[...], up[:main, :])
    active[:, :main] = (g / (1.0 + jnp.exp(-g)) * u).astype(BF)
    rest = product(x[...], jnp.concatenate([gate[main:, :], up[main:, :]], axis=0))
    g, u = rest[:, : hidden - main], rest[:, hidden - main :]
    active[:, main:] = (g / (1.0 + jnp.exp(-g)) * u).astype(BF)
    step = 512

    @pl.loop(0, width // step)
    def _(j):
        cols = pl.ds(pl.multiple_of(j * step, step), step)
        y[:, cols] = jnp.dot(active[...], down[:, cols], preferred_element_type=F32).astype(BF)

    stores = [
        pltpu.make_async_copy(y.at[pl.ds(starts[i], sizes[i])], outs[i], sem_y.at[i])
        for i in range(n)
    ]
    for copy in stores:
        copy.start()
    for copy in stores:
        copy.wait()


def ffn(pieces, gate, up, down):
    held, sources, sizes = [], [], []
    for piece in pieces:
        array, at, size = piece if isinstance(piece, tuple) else (piece, 0, piece.shape[0])
        if not any(array is other for other in held):
            held.append(array)
        sources.append(([array is other for other in held].index(True), at))
        sizes.append(size)
    total, n = sum(sizes), len(sizes)
    hidden, width = gate.shape
    moved = 2 * (2 * total * width + 3 * hidden * width)
    return pl.pallas_call(
        functools.partial(ffn_kernel, sources, sizes),
        out_shape=[jax.ShapeDtypeStruct((size, width), BF) for size in sizes],
        in_specs=[pl.BlockSpec(memory_space=pl.ANY)] * len(held)
        + [pl.BlockSpec(memory_space=pltpu.VMEM)] * 3,
        out_specs=[pl.BlockSpec(memory_space=pl.ANY)] * n,
        scratch_shapes=[
            pltpu.VMEM((total, width), BF),
            pltpu.VMEM((total, hidden), BF),
            pltpu.VMEM((total, width), BF),
            pltpu.SemaphoreType.DMA((n,)),
            pltpu.SemaphoreType.DMA((n,)),
        ],
        compiler_params=pltpu.CompilerParams(vmem_limit_bytes=32 * 2**20),
        cost_estimate=pl.CostEstimate(
            flops=6 * total * width * hidden, bytes_accessed=moved, transcendentals=total * hidden
        ),
    )(*held, gate, up, down)


def cat(*pieces):
    return jnp.concatenate(pieces, axis=0)


def gather_compute_reduce(rows, gate, up, down):
    a, b = rows[:16], rows[16:]
    am, ap, a2 = shift_x(a, 1), shift_x(a, -1), shift_x(a, 2)
    b1m, b1p = shift_z(b, 1), shift_z(b, -1)
    am, ap, a2, b1m, b1p = lax.optimization_barrier((am, ap, a2, b1m, b1p))
    a0 = cat(a, am, ap, a2)
    zm, zp = shift_z(cat(a0, b1m), 1), shift_z(cat(b1p, a0), -1)
    x1 = cat(b, b1m, b1p)
    x1m, x1p = shift_x(x1, 1), shift_x(x1, -1)
    z1m, z1p = zm, zp
    zm, zp = shift_z(z1m, 1), shift_z(z1p, -1)
    x2 = cat(z1m[64:], z1p[:32])
    x2m, x2p = shift_x(cat(x2, x1m[:48]), 1), shift_x(cat(x2, x1p[48:]), -1)
    out_1 = ffn(
        (a0, (z1m, 0, 64), (z1p, 32, 64), x1, x1m, x1p), gate, up, down
    )
    z2m, z2p = zm, zp
    z2m, z2p, x2m, x2p, out_1 = lax.optimization_barrier((z2m, z2p, x2m, x2p, out_1))
    zm, zp = shift_z(z2m[:80], 1), shift_z(z2p[16:], -1)
    x3 = cat(z2m[64:], z2p[:32])
    x3m, x3p = shift_x(cat(x3, x2m[:32]), 1), shift_x(cat(x3, x2p[32:64]), -1)
    out_2 = ffn(
        (
            (z2m, 0, 64),
            (z2p, 32, 64),
            x2,
            (x2m, 0, 64),
            (x2p, 0, 64),
            (x2m, 64, 48),
            (x2p, 64, 48),
        ),
        gate,
        up,
        down,
    )
    z3m, z3p = zm, zp
    z3m, z3p, x3m, x3p, out_2 = lax.optimization_barrier((z3m, z3p, x3m, x3p, out_2))
    z4m, z4p = shift_z(z3m[:32], 1), shift_z(z3p[48:], -1)
    x4 = cat(z3m[64:], z3p[:16])
    x4m = shift_x(cat(x4, x3m[:32], out_2[6]), 1)
    x4p = shift_x(cat(x4, x3p[32:64], out_2[5]), -1)
    out_3 = ffn(
        (
            (z3m, 0, 64),
            (z3p, 16, 64),
            x4,
            x3,
            (x3m, 0, 64),
            (x3p, 0, 64),
            (x3m, 64, 32),
            (x3p, 64, 32),
        ),
        gate,
        up,
        down,
    )
    z4m, z4p, x4m, x4p, out_3 = lax.optimization_barrier((z4m, z4p, x4m, x4p, out_3))
    x5m, x5p = shift_x(x4m[:16], 1), shift_x(x4p[16:32], -1)
    c1m, c1p = plus_head(out_1[4], x4p[64:]), plus_tail(out_1[5], x4m[64:])
    c1m, c1p, z4m, z4p = lax.optimization_barrier((c1m, c1p, z4m, z4p))
    c1m, c1p = shift_x(c1m, -1), shift_x(c1p, 1)
    out_4 = ffn(
        (z4m, z4p, (x4m, 0, 32), (x4p, 0, 32), (x4m, 32, 32), (x4p, 32, 32)), gate, up, down
    )
    x5m, x5p, out_4 = lax.optimization_barrier((x5m, x5p, out_4))
    out_5 = ffn((x5m, x5p), gate, up, down)

    a0, a1m, a1p, x1 = out_1[:4]
    a2m, a2p, x2, x2m, x2p = out_2[:5]
    a3m, a3p, x4, x3, x3m, x3p, x2m2, x2p2 = out_3
    a4m, a4p, x4m, x4p, x3m2, x3p2 = out_4
    x5m, x5p = out_5
    zm, zp = shift_z(a4m, -1), shift_z(a4p, 1)
    zm, zp, x5m, x5p = lax.optimization_barrier((zm, zp, x5m, x5p))
    xm, xp = shift_x(x5m, -1), shift_x(x5p, 1)
    xm, xp, c1m, c1p = lax.optimization_barrier((xm, xp, c1m, c1p))
    zm, zp = shift_z(plus_head(a3m, zm), -1), shift_z(plus_tail(a3p, zp), 1)
    xm = shift_x(cat(plus_head(x4m, xm), x3m2), -1)
    xp = shift_x(cat(plus_tail(x4p, xp), x3p2), 1)
    zm, zp, xm, xp = lax.optimization_barrier((zm, zp, xm, xp))
    (c4m, h3m), (c4p, h3p) = cut(xm, (32, 32)), cut(xp, (32, 32))
    b4m, b4p = cut(plus3(x4, c4m, c4p), (16, 16))
    zm, zp = shift_z(cat(plus(a2m, zm), b4m), -1), shift_z(cat(b4p, plus(a2p, zp)), 1)
    xm = shift_x(cat(plus_head(x3m, h3m), x2m2), -1)
    xp = shift_x(cat(plus_tail(x3p, h3p), x2p2), 1)
    zm, zp, xm, xp = lax.optimization_barrier((zm, zp, xm, xp))
    (c3m, h2m), (c3p, h2p) = cut(xm, (64, 32)), cut(xp, (64, 32))
    b3m, b3p = cut(plus3(x3, c3m, c3p), (32, 32))
    (zm, d4m), (d4p, zp) = cut(zm, (64, 16)), cut(zp, (16, 64))
    zm = shift_z(cat(plus(a1m, zm), plus_head(b3m, d4m)), -1)
    zp = shift_z(cat(plus_tail(b3p, d4p), plus(a1p, zp)), 1)
    c2m, c2p = shift_x(plus_head(x2m, h2m), -1), shift_x(plus_tail(x2p, h2p), 1)
    b, b1m, b1p = cut(plus3(x1, c1m, c1p), (32, 32, 32))
    zm, zp, c2m, c2p, b = lax.optimization_barrier((zm, zp, c2m, c2p, b))
    b2m, b2p = cut(plus3(x2, c2m, c2p), (32, 32))
    (zm, d3m), (d3p, zp) = cut(zm, (64, 32)), cut(zp, (32, 64))
    d2m, d2p = shift_z(plus(b2m, d3m), -1), shift_z(plus(b2p, d3p), 1)
    a, am, ap, a2 = cut(plus3(a0, zm, zp), (16, 16, 16, 16))
    am, ap, a2 = shift_x(am, -1), shift_x(ap, 1), shift_x(a2, 2)
    d1m, d1p = shift_z(plus(b1m, d2m), -1), shift_z(plus(b1p, d2p), 1)
    a_sum = a.astype(F32) + am.astype(F32) + ap.astype(F32) + a2.astype(F32)
    b_sum = b.astype(F32) + d1m.astype(F32) + d1p.astype(F32)
    return a_sum, b_sum


def parts_of_log(total):
    first = lax.reduce_precision(total, 8, 7)
    second = lax.reduce_precision(total - first, 8, 7)
    third = total - first - second
    return first.astype(BF), second.astype(BF), third.astype(BF)


def carried_state(block_total, block_state):
    heads = block_total.shape[0]
    seqs = lax.axis_size("seq")
    state = block_state.astype(BF).reshape(seqs, -1, 128)
    each = state.shape[1]
    marks = jnp.stack(parts_of_log(block_total), axis=0)
    marks = jnp.repeat(marks, seqs // heads, axis=1).T
    marks = jnp.broadcast_to(marks[:, :, None], (seqs, 3, 128))
    marks = jnp.concatenate([marks, jnp.zeros((seqs, 5, 128), BF)], axis=1)
    sent = jnp.concatenate([state, marks], axis=1)
    got = lax.all_to_all(sent, "seq", split_axis=0, concat_axis=0, tiled=True)
    totals = jnp.sum(got[:, each : each + 3, 0].astype(F32), axis=1)
    row = lax.broadcasted_iota(jnp.int32, (seqs, seqs), 0)
    col = lax.broadcasted_iota(jnp.int32, (seqs, seqs), 1)
    upto = jnp.sum(jnp.where(row >= col, totals[None, :], 0.0), axis=1)
    before = upto - totals
    gap = jnp.where(row > col, before[:, None] - upto[None, :], 0.0)
    weight = jnp.where(row > col, jnp.exp(gap), 0.0)
    states = got[:, :each, :].reshape(seqs, -1).astype(F32)
    summed = jnp.dot(weight, states, precision=lax.Precision.HIGHEST).astype(BF)
    back = lax.all_to_all(
        summed.reshape(seqs, each, 128), "seq", split_axis=0, concat_axis=0, tiled=True
    )
    return back.reshape(heads, 128, 128)


def route_targets(ids_block, experts):
    flat_ids = ids_block.reshape(-1)
    onehot = (flat_ids[:, None] == jnp.arange(experts, dtype=jnp.int32)[None, :]).astype(F32)
    n = flat_ids.shape[0]
    earlier = (jnp.arange(n)[:, None] > jnp.arange(n)[None, :]).astype(F32)
    before = jnp.dot(earlier, onehot, preferred_element_type=F32)
    slot = jnp.sum(before * onehot, axis=1).astype(jnp.int32)
    return flat_ids * CAP + slot


def body(
    queries,
    keys,
    values,
    log_decay,
    residual,
    attn_gain,
    moe_gain,
    expert_ids,
    gate_weights,
    w_gate,
    w_up,
    w_down,
):
    rows = queries.shape[0]
    heads = log_decay.shape[1]
    hd = queries.shape[1] // heads
    exps = lax.axis_size("exp")
    tok_rows, width = residual.shape
    share = width // exps
    place = lax.axis_index("exp")

    slots = exps * CAP
    target = route_targets(expert_ids, exps).reshape(tok_rows, 2)
    marked = jnp.concatenate(
        [residual, jnp.pad(target.astype(BF), ((0, 0), (0, 126)))], axis=1
    )
    block_tokens = lax.all_gather(marked, "exp", axis=0, tiled=True)
    res_cols = lax.dynamic_slice_in_dim(block_tokens, place * share, share, axis=1)
    targets = block_tokens[:, width : width + 2].astype(jnp.int32).reshape(exps, tok_rows, 2)
    gain_cols = lax.dynamic_slice_in_dim(attn_gain, place * share, share, axis=0)

    q_heads = queries.reshape(rows, heads, hd)
    k_heads = keys.reshape(rows, heads, hd)
    v_heads = values.reshape(rows, heads, hd)
    causal = lax.broadcasted_iota(jnp.int32, (rows, rows), 0) >= lax.broadcasted_iota(
        jnp.int32, (rows, rows), 1
    )
    log_cum = jnp.dot(causal.astype(F32), log_decay, precision=lax.Precision.HIGHEST)
    block_total = log_cum[-1]
    keys_weighted = (k_heads * jnp.exp(block_total[None, :] - log_cum)[:, :, None]).astype(BF)
    block_state = jnp.einsum("thd,the->hde", keys_weighted, v_heads, preferred_element_type=F32)
    carried = carried_state(block_total, block_state)
    scores = jnp.einsum("thd,shd->hts", q_heads, k_heads, preferred_element_type=F32)
    gap_logs = log_cum.T[:, :, None] - log_cum.T[:, None, :]
    mask = causal[None, :, :]
    weights = jnp.where(mask, scores * jnp.exp(jnp.where(mask, gap_logs, 0.0)), 0.0).astype(BF)
    intra = jnp.einsum("hts,she->the", weights, v_heads, preferred_element_type=F32)
    inter = jnp.exp(log_cum)[:, :, None] * jnp.einsum(
        "thd,hde->the", q_heads, carried, preferred_element_type=F32
    )
    attn = intra + inter
    normed = (attn * lax.rsqrt(jnp.mean(attn * attn, axis=-1, keepdims=True) + 1e-06)).astype(BF)
    normed = normed.reshape(rows, heads * hd)
    hidden_cols = (res_cols.astype(F32) + normed.astype(F32) * gain_cols[None, :]).astype(BF)

    slot_range = jnp.arange(slots, dtype=jnp.int32)
    hit = jnp.any(targets[:, None, :, :] == slot_range[None, :, None, None], axis=3)
    picker = hit.astype(BF)
    outgoing = jnp.einsum(
        "jkt,jtd->kjd",
        picker,
        hidden_cols.reshape(exps, tok_rows, share),
        preferred_element_type=F32,
    ).astype(BF)
    outgoing = outgoing.reshape(exps, CAP * exps, share)
    arrived = lax.all_to_all(outgoing, "exp", split_axis=0, concat_axis=0, tiled=True)
    hid_rows = arrived.transpose(1, 0, 2).reshape(slots, width)
    hid32_rows = hid_rows.astype(F32)
    moe_rows = (
        hid32_rows
        * lax.rsqrt(jnp.mean(hid32_rows * hid32_rows, axis=-1, keepdims=True) + 1e-06)
        * moe_gain
    ).astype(BF)

    hidden_all = lax.all_gather(hidden_cols, "exp", axis=0, tiled=False)
    hidden_own = lax.dynamic_slice_in_dim(hidden_all, place * tok_rows, tok_rows, axis=1)
    hidden_own = hidden_own.transpose(1, 0, 2).reshape(tok_rows, width)

    expert_sums = gather_compute_reduce(moe_rows, w_gate[0], w_up[0], w_down[0])
    expert_rows = jnp.concatenate(expert_sums, axis=0).astype(BF)

    by_block = expert_rows.reshape(CAP, exps, width).transpose(1, 0, 2)
    returned = lax.all_to_all(by_block, "exp", split_axis=0, concat_axis=0, tiled=True)
    flat_back = returned.reshape(slots, width)
    chosen = (target[:, :, None] == slot_range[None, None, :]).astype(BF)
    picked = jnp.einsum("trk,kd->trd", chosen, flat_back, preferred_element_type=F32)
    mixed = hidden_own.astype(F32) + jnp.sum(gate_weights[:, :, None] * picked, axis=1)
    return mixed.astype(BF)


def solution(mesh):
    in_specs = (
        P("seq", "exp"),
        P("seq", "exp"),
        P("seq", "exp"),
        P("seq", "exp"),
        P(("seq", "exp"), None),
        P(),
        P(),
        P(("seq", "exp"), None),
        P(("seq", "exp"), None),
        P("exp", "seq", None),
        P("exp", "seq", None),
        P("exp", "seq", None),
    )
    out_specs = P(("seq", "exp"), None)
    return jax.shard_map(body, mesh=mesh, in_specs=in_specs, out_specs=out_specs, check_vma=False)
```

```python
import functools

import jax
import jax.numpy as jnp
from jax import lax
from jax.experimental import pallas as pl
from jax.experimental.pallas import tpu as pltpu
from jax.sharding import PartitionSpec as P

BF = jnp.bfloat16
F32 = jnp.float32
NX, NZ = 4, 8
CAP = 6


def shift_x(value, by):
    pairs = [(x * NZ + z, ((x + by) % NX) * NZ + z) for x in range(NX) for z in range(NZ)]
    return lax.ppermute(value, "seq", pairs)


def shift_z(value, by):
    pairs = [(x * NZ + z, x * NZ + (z + by) % NZ) for x in range(NX) for z in range(NZ)]
    return lax.ppermute(value, "seq", pairs)


def butterfly(blocks, axis):
    n = blocks.shape[0]
    place = lax.axis_index(axis)
    step = 1
    while step < n:
        split = blocks.reshape((n // (2 * step), 2, step) + blocks.shape[1:])
        low, high = split[:, 0], split[:, 1]
        upper = (place // step) % 2 == 1
        got = lax.ppermute(jnp.where(upper, low, high), axis, [(i, i ^ step) for i in range(n)])
        low, high = jnp.where(upper, got, low), jnp.where(upper, high, got)
        blocks = jnp.stack([low, high], axis=1).reshape(blocks.shape)
        step *= 2
    return blocks


def added(rows, *parts):
    total = 0.0
    for part, at in parts:
        after = rows - at - part.shape[0]
        total = total + jnp.pad(part.astype(F32), ((at, after), (0, 0)))
    return total.astype(BF)


def ffn_kernel(sources, sizes, *refs):
    n, given = len(sizes), max(which for which, _ in sources) + 1
    held, (gate, up, down) = refs[:given], refs[given : given + 3]
    outs = refs[given + 3 : given + 3 + n]
    x, active, y, sem_x, sem_y = refs[given + 3 + n :]
    pieces = [held[which].at[pl.ds(at, size)] for (which, at), size in zip(sources, sizes)]
    hidden, width = gate.shape
    main = hidden // 256 * 256
    starts = [sum(sizes[:i]) for i in range(n)]
    loads = [
        pltpu.make_async_copy(pieces[i], x.at[pl.ds(starts[i], sizes[i])], sem_x.at[i])
        for i in range(n)
    ]
    for copy in loads:
        copy.start()
    for copy in loads:
        copy.wait()

    def product(rows, block):
        return lax.dot_general(
            rows, block, (((1,), (1,)), ((), ())), preferred_element_type=F32
        )

    g = product(x[...], gate[:main, :])
    u = product(x[...], up[:main, :])
    active[:, :main] = (g / (1.0 + jnp.exp(-g)) * u).astype(BF)
    rest = product(x[...], jnp.concatenate([gate[main:, :], up[main:, :]], axis=0))
    g, u = rest[:, : hidden - main], rest[:, hidden - main :]
    active[:, main:] = (g / (1.0 + jnp.exp(-g)) * u).astype(BF)
    step = 512

    @pl.loop(0, width // step)
    def _(j):
        cols = pl.ds(pl.multiple_of(j * step, step), step)
        y[:, cols] = jnp.dot(active[...], down[:, cols], preferred_element_type=F32).astype(BF)

    stores = [
        pltpu.make_async_copy(y.at[pl.ds(starts[i], sizes[i])], outs[i], sem_y.at[i])
        for i in range(n)
    ]
    for copy in stores:
        copy.start()
    for copy in stores:
        copy.wait()


def ffn(pieces, gate, up, down):
    held, sources, sizes = [], [], []
    for piece in pieces:
        array, at, size = piece if isinstance(piece, tuple) else (piece, 0, piece.shape[0])
        if not any(array is other for other in held):
            held.append(array)
        sources.append(([array is other for other in held].index(True), at))
        sizes.append(size)
    total, n = sum(sizes), len(sizes)
    hidden, width = gate.shape
    moved = 2 * (2 * total * width + 3 * hidden * width)
    return pl.pallas_call(
        functools.partial(ffn_kernel, sources, sizes),
        out_shape=[jax.ShapeDtypeStruct((size, width), BF) for size in sizes],
        in_specs=[pl.BlockSpec(memory_space=pl.ANY)] * len(held)
        + [pl.BlockSpec(memory_space=pltpu.VMEM)] * 3,
        out_specs=[pl.BlockSpec(memory_space=pl.ANY)] * n,
        scratch_shapes=[
            pltpu.VMEM((total, width), BF),
            pltpu.VMEM((total, hidden), BF),
            pltpu.VMEM((total, width), BF),
            pltpu.SemaphoreType.DMA((n,)),
            pltpu.SemaphoreType.DMA((n,)),
        ],
        compiler_params=pltpu.CompilerParams(vmem_limit_bytes=32 * 2**20),
        cost_estimate=pl.CostEstimate(
            flops=6 * total * width * hidden, bytes_accessed=moved, transcendentals=total * hidden
        ),
    )(*held, gate, up, down)


def cat(*pieces):
    return jnp.concatenate(pieces, axis=0)


def gather_compute_reduce(rows, gate, up, down, hidden_cols):
    a, b = rows[:16], rows[16:]
    am, ap, a2 = shift_x(a, 1), shift_x(a, -1), shift_x(a, 2)
    b1m, b1p = shift_z(b, 1), shift_z(b, -1)
    am, ap, a2, b1m, b1p, hidden_cols = lax.optimization_barrier((am, ap, a2, b1m, b1p, hidden_cols))
    hidden_own = lax.all_to_all(hidden_cols, "exp", split_axis=0, concat_axis=0, tiled=True)
    a0 = cat(a, am, ap, a2)
    zm, zp = shift_z(cat(a0, b1m), 1), shift_z(cat(b1p, a0), -1)
    x1 = cat(b, b1m, b1p)
    x1m, x1p = shift_x(x1, 1), shift_x(x1, -1)
    z1m, z1p = zm, zp
    zm, zp = shift_z(z1m, 1), shift_z(z1p, -1)
    x2 = cat(z1m[64:], z1p[:32])
    x2m, x2p = shift_x(cat(x2, x1m[:48]), 1), shift_x(cat(x2, x1p[48:]), -1)
    out_1 = ffn(
        (a0, (z1m, 0, 64), (z1p, 32, 64), x1, x1m, x1p), gate, up, down
    )
    z2m, z2p = zm, zp
    z2m, z2p, x2m, x2p, out_1, hidden_own = lax.optimization_barrier(
        (z2m, z2p, x2m, x2p, out_1, hidden_own)
    )
    hidden_own = hidden_own.transpose(1, 0, 2).reshape(hidden_own.shape[1], -1)
    zm, zp = shift_z(z2m[:80], 1), shift_z(z2p[16:], -1)
    x3 = cat(z2m[64:], z2p[:32])
    x3m, x3p = shift_x(cat(x3, x2m[:32]), 1), shift_x(cat(x3, x2p[32:64]), -1)
    out_2 = ffn(
        (
            (z2m, 0, 64),
            (z2p, 32, 64),
            x2,
            (x2m, 0, 64),
            (x2p, 0, 64),
            (x2m, 64, 48),
            (x2p, 64, 48),
        ),
        gate,
        up,
        down,
    )
    z3m, z3p = zm, zp
    z3m, z3p, x3m, x3p, out_2 = lax.optimization_barrier((z3m, z3p, x3m, x3p, out_2))
    z4m, z4p = shift_z(z3m[:32], 1), shift_z(z3p[48:], -1)
    x4 = cat(z3m[64:], z3p[:16])
    x4m = shift_x(cat(x4, x3m[:32], out_2[6]), 1)
    x4p = shift_x(cat(x4, x3p[32:64], out_2[5]), -1)
    out_3 = ffn(
        (
            (z3m, 0, 64),
            (z3p, 16, 64),
            x4,
            x3,
            x3m,
            x3p,
        ),
        gate,
        up,
        down,
    )
    z4m, z4p, x4m, x4p, out_3 = lax.optimization_barrier((z4m, z4p, x4m, x4p, out_3))
    x5m, x5p = shift_x(x4m[:16], 1), shift_x(x4p[16:32], -1)
    out_4 = ffn((z4m, z4p, (x4m, 0, 64), (x4p, 0, 64)), gate, up, down)
    h1m, h1p = x4p[64:], x4m[64:]
    x5m, x5p, out_4 = lax.optimization_barrier((x5m, x5p, out_4))
    out_5 = ffn((x5m, x5p), gate, up, down)

    a0, a1m, a1p, x1, x1m, x1p = out_1
    a2m, a2p, x2, x2m, x2p = out_2[:5]
    a3m, a3p, x4, x3, x3m, x3p = out_3
    a4m, a4p, x4m, x4p = out_4
    x5m, x5p = out_5
    zm, zp = shift_z(a4m, -1), shift_z(a4p, 1)
    xm, xp = shift_x(x5m, -1), shift_x(x5p, 1)
    x1m, x1p = added(96, (x1m, 0), (h1m, 0)), added(96, (x1p, 0), (h1p, 48))
    zm = shift_z(added(64, (a3m, 0), (zm, 0)), -1)
    zp = shift_z(added(64, (a3p, 0), (zp, 32)), 1)
    xm = shift_x(added(64, (x4m, 0), (xm, 0)), -1)
    xp = shift_x(added(64, (x4p, 0), (xp, 16)), 1)
    b4 = added(32, (x4, 0), (xm[:32], 0), (xp[:32], 0))
    zm = shift_z(added(80, (a2m, 0), (zm, 0), (b4[:16], 64)), -1)
    zp = shift_z(added(80, (a2p, 16), (zp, 16), (b4[16:], 0)), 1)
    xm = shift_x(added(96, (x3m, 0), (xm[32:], 0)), -1)
    xp = shift_x(added(96, (x3p, 0), (xp[32:], 32)), 1)
    b3 = added(64, (x3, 0), (xm[:64], 0), (xp[:64], 0))
    zm = shift_z(added(96, (a1m, 0), (zm, 0), (b3[:32], 64)), -1)
    zp = shift_z(added(96, (a1p, 32), (zp, 16), (b3[32:], 0)), 1)
    xm = shift_x(added(96, (x2m, 0), (xm[64:], 0), (x1m[:32], 64)), -1)
    xp = shift_x(added(96, (x2p, 0), (xp[64:], 32), (x1p[:32], 64)), 1)
    b2 = added(64, (x2, 0), (xm[:64], 0), (xp[:64], 0))
    b = added(32, (x1[:32], 0), (xm[64:], 0), (xp[64:], 0))
    a = added(64, (a0, 0), (zm[:64], 0), (zp[32:], 0))
    zm = shift_z(added(32, (b2[:32], 0), (zm[64:], 0)), -1)
    zp = shift_z(added(32, (b2[32:], 0), (zp[:32], 0)), 1)
    xm, xp = shift_x(cat(x1m[32:], a[16:32]), -1), shift_x(cat(x1p[32:], a[32:48]), 1)
    a2 = shift_x(a[48:], 2)
    b1 = added(64, (x1[32:], 0), (xm[:64], 0), (xp[:64], 0))
    zm = shift_z(added(32, (b1[:32], 0), (zm, 0)), -1)
    zp = shift_z(added(32, (b1[32:], 0), (zp, 0)), 1)
    a_sum = added(16, (a[:16], 0), (xm[64:], 0), (xp[64:], 0), (a2, 0))
    b_sum = added(32, (b, 0), (zm, 0), (zp, 0))
    return (a_sum, b_sum), hidden_own


def parts_of_log(total):
    first = lax.reduce_precision(total, 8, 7)
    second = lax.reduce_precision(total - first, 8, 7)
    third = total - first - second
    return first.astype(BF), second.astype(BF), third.astype(BF)


def carried_state(block_total, block_state):
    heads = block_total.shape[0]
    seqs = lax.axis_size("seq")
    state = block_state.astype(BF).reshape(seqs, -1, 128)
    each = state.shape[1]
    marks = jnp.stack(parts_of_log(block_total), axis=0)
    marks = jnp.repeat(marks, seqs // heads, axis=1).T
    marks = jnp.broadcast_to(marks[:, :, None], (seqs, 3, 128))
    marks = jnp.concatenate([marks, jnp.zeros((seqs, 5, 128), BF)], axis=1)
    sent = jnp.concatenate([state, marks], axis=1)
    got = lax.all_to_all(sent, "seq", split_axis=0, concat_axis=0, tiled=True)
    totals = jnp.sum(got[:, each : each + 3, 0].astype(F32), axis=1)
    row = lax.broadcasted_iota(jnp.int32, (seqs, seqs), 0)
    col = lax.broadcasted_iota(jnp.int32, (seqs, seqs), 1)
    upto = jnp.sum(jnp.where(row >= col, totals[None, :], 0.0), axis=1)
    before = upto - totals
    gap = jnp.where(row > col, before[:, None] - upto[None, :], 0.0)
    weight = jnp.where(row > col, jnp.exp(gap), 0.0)
    states = got[:, :each, :].reshape(seqs, -1).astype(F32)
    summed = jnp.dot(weight, states, precision=lax.Precision.HIGHEST).astype(BF)
    back = lax.all_to_all(
        summed.reshape(seqs, each, 128), "seq", split_axis=0, concat_axis=0, tiled=True
    )
    return back.reshape(heads, 128, 128)


def route_targets(ids_block, experts):
    flat_ids = ids_block.reshape(-1)
    onehot = (flat_ids[:, None] == jnp.arange(experts, dtype=jnp.int32)[None, :]).astype(F32)
    n = flat_ids.shape[0]
    earlier = (jnp.arange(n)[:, None] > jnp.arange(n)[None, :]).astype(F32)
    before = jnp.dot(earlier, onehot, preferred_element_type=F32)
    slot = jnp.sum(before * onehot, axis=1).astype(jnp.int32)
    return flat_ids * CAP + slot


def body(
    queries,
    keys,
    values,
    log_decay,
    residual,
    attn_gain,
    moe_gain,
    expert_ids,
    gate_weights,
    w_gate,
    w_up,
    w_down,
):
    rows = queries.shape[0]
    heads = log_decay.shape[1]
    hd = queries.shape[1] // heads
    exps = lax.axis_size("exp")
    tok_rows, width = residual.shape
    share = width // exps
    place = lax.axis_index("exp")

    slots = exps * CAP
    target = route_targets(expert_ids, exps).reshape(tok_rows, 2)
    marked = jnp.concatenate(
        [
            residual.reshape(tok_rows, exps, share).transpose(1, 0, 2),
            jnp.broadcast_to(
                jnp.pad(target.astype(BF), ((0, 0), (0, 126)))[None], (exps, tok_rows, 128)
            ),
        ],
        axis=2,
    )
    block_tokens = butterfly(marked, "exp")
    block_tokens = block_tokens.reshape(exps * tok_rows, share + 128)
    res_cols = block_tokens[:, :share]
    targets = block_tokens[:, share : share + 2].astype(jnp.int32).reshape(exps, tok_rows, 2)
    gain_cols = lax.dynamic_slice_in_dim(attn_gain, place * share, share, axis=0)

    q_heads = queries.reshape(rows, heads, hd)
    k_heads = keys.reshape(rows, heads, hd)
    v_heads = values.reshape(rows, heads, hd)
    causal = lax.broadcasted_iota(jnp.int32, (rows, rows), 0) >= lax.broadcasted_iota(
        jnp.int32, (rows, rows), 1
    )
    log_cum = jnp.dot(causal.astype(F32), log_decay, precision=lax.Precision.HIGHEST)
    block_total = log_cum[-1]
    keys_weighted = (k_heads * jnp.exp(block_total[None, :] - log_cum)[:, :, None]).astype(BF)
    block_state = jnp.einsum("thd,the->hde", keys_weighted, v_heads, preferred_element_type=F32)
    carried = carried_state(block_total, block_state)
    scores = jnp.einsum("thd,shd->hts", q_heads, k_heads, preferred_element_type=F32)
    gap_logs = log_cum.T[:, :, None] - log_cum.T[:, None, :]
    mask = causal[None, :, :]
    weights = jnp.where(mask, scores * jnp.exp(jnp.where(mask, gap_logs, 0.0)), 0.0).astype(BF)
    intra = jnp.einsum("hts,she->the", weights, v_heads, preferred_element_type=F32)
    inter = jnp.exp(log_cum)[:, :, None] * jnp.einsum(
        "thd,hde->the", q_heads, carried, preferred_element_type=F32
    )
    attn = intra + inter
    normed = (attn * lax.rsqrt(jnp.mean(attn * attn, axis=-1, keepdims=True) + 1e-06)).astype(BF)
    normed = normed.reshape(rows, heads * hd)
    hidden_cols = (res_cols.astype(F32) + normed.astype(F32) * gain_cols[None, :]).astype(BF)

    slot_range = jnp.arange(slots, dtype=jnp.int32)
    hit = jnp.any(targets[:, None, :, :] == slot_range[None, :, None, None], axis=3)
    picker = hit.astype(BF)
    outgoing = jnp.einsum(
        "jkt,jtd->kjd",
        picker,
        hidden_cols.reshape(exps, tok_rows, share),
        preferred_element_type=F32,
    ).astype(BF)
    outgoing = outgoing.reshape(exps, CAP * exps, share)
    arrived = lax.all_to_all(outgoing, "exp", split_axis=0, concat_axis=0, tiled=True)
    hid_rows = arrived.transpose(1, 0, 2).reshape(slots, width)
    hid32_rows = hid_rows.astype(F32)
    moe_rows = (
        hid32_rows
        * lax.rsqrt(jnp.mean(hid32_rows * hid32_rows, axis=-1, keepdims=True) + 1e-06)
        * moe_gain
    ).astype(BF)

    expert_sums, hidden_own = gather_compute_reduce(
        moe_rows, w_gate[0], w_up[0], w_down[0], hidden_cols.reshape(exps, tok_rows, share)
    )
    expert_rows = jnp.concatenate(expert_sums, axis=0).astype(BF)

    by_block = expert_rows.reshape(CAP, exps, width).transpose(1, 0, 2)
    returned = lax.all_to_all(by_block, "exp", split_axis=0, concat_axis=0, tiled=True)
    flat_back = returned.reshape(slots, width)
    chosen = (target[:, :, None] == slot_range[None, None, :]).astype(BF)
    picked = jnp.einsum("trk,kd->trd", chosen, flat_back, preferred_element_type=F32)
    mixed = hidden_own.astype(F32) + jnp.sum(gate_weights[:, :, None] * picked, axis=1)
    return mixed.astype(BF)


def solution(mesh):
    in_specs = (
        P("seq", "exp"),
        P("seq", "exp"),
        P("seq", "exp"),
        P("seq", "exp"),
        P(("seq", "exp"), None),
        P(),
        P(),
        P(("seq", "exp"), None),
        P(("seq", "exp"), None),
        P("exp", "seq", None),
        P("exp", "seq", None),
        P("exp", "seq", None),
    )
    out_specs = P(("seq", "exp"), None)
    return jax.shard_map(body, mesh=mesh, in_specs=in_specs, out_specs=out_specs, check_vma=False)
```

```python
import functools

import jax
import jax.numpy as jnp
from jax import lax
from jax.experimental import pallas as pl
from jax.experimental.pallas import tpu as pltpu
from jax.sharding import PartitionSpec as P

BF = jnp.bfloat16
F32 = jnp.float32
NX, NZ = 4, 8
CAP = 6


def shift_x(value, by):
    pairs = [(x * NZ + z, ((x + by) % NX) * NZ + z) for x in range(NX) for z in range(NZ)]
    return lax.ppermute(value, "seq", pairs)


def shift_z(value, by):
    pairs = [(x * NZ + z, x * NZ + (z + by) % NZ) for x in range(NX) for z in range(NZ)]
    return lax.ppermute(value, "seq", pairs)


def butterfly(blocks, axis):
    n = blocks.shape[0]
    place = lax.axis_index(axis)
    step = 1
    while step < n:
        split = blocks.reshape((n // (2 * step), 2, step) + blocks.shape[1:])
        low, high = split[:, 0], split[:, 1]
        upper = (place // step) % 2 == 1
        got = lax.ppermute(jnp.where(upper, low, high), axis, [(i, i ^ step) for i in range(n)])
        low, high = jnp.where(upper, got, low), jnp.where(upper, high, got)
        blocks = jnp.stack([low, high], axis=1).reshape(blocks.shape)
        step *= 2
    return blocks


def added(rows, *parts):
    total = 0.0
    for part, at in parts:
        after = rows - at - part.shape[0]
        total = total + jnp.pad(part.astype(F32), ((at, after), (0, 0)))
    return total.astype(BF)


def ffn_kernel(sources, sizes, *refs):
    n, given = len(sizes), max(which for which, _ in sources) + 1
    held, (gate, up, down) = refs[:given], refs[given : given + 3]
    outs = refs[given + 3 : given + 3 + n]
    x, active, y, sem_x, sem_y = refs[given + 3 + n :]
    pieces = [held[which].at[pl.ds(at, size)] for (which, at), size in zip(sources, sizes)]
    hidden, width = gate.shape
    main = hidden // 256 * 256
    starts = [sum(sizes[:i]) for i in range(n)]
    loads = [
        pltpu.make_async_copy(pieces[i], x.at[pl.ds(starts[i], sizes[i])], sem_x.at[i])
        for i in range(n)
    ]
    for copy in loads:
        copy.start()
    for copy in loads:
        copy.wait()

    def product(rows, block):
        return lax.dot_general(
            rows, block, (((1,), (1,)), ((), ())), preferred_element_type=F32
        )

    g = product(x[...], gate[:main, :])
    u = product(x[...], up[:main, :])
    active[:, :main] = (g / (1.0 + jnp.exp(-g)) * u).astype(BF)
    rest = product(x[...], jnp.concatenate([gate[main:, :], up[main:, :]], axis=0))
    g, u = rest[:, : hidden - main], rest[:, hidden - main :]
    active[:, main:] = (g / (1.0 + jnp.exp(-g)) * u).astype(BF)
    step = 512

    @pl.loop(0, width // step)
    def _(j):
        cols = pl.ds(pl.multiple_of(j * step, step), step)
        y[:, cols] = jnp.dot(active[...], down[:, cols], preferred_element_type=F32).astype(BF)

    stores = [
        pltpu.make_async_copy(y.at[pl.ds(starts[i], sizes[i])], outs[i], sem_y.at[i])
        for i in range(n)
    ]
    for copy in stores:
        copy.start()
    for copy in stores:
        copy.wait()


def ffn(pieces, gate, up, down):
    held, sources, sizes = [], [], []
    for piece in pieces:
        array, at, size = piece if isinstance(piece, tuple) else (piece, 0, piece.shape[0])
        if not any(array is other for other in held):
            held.append(array)
        sources.append(([array is other for other in held].index(True), at))
        sizes.append(size)
    total, n = sum(sizes), len(sizes)
    hidden, width = gate.shape
    moved = 2 * (2 * total * width + 3 * hidden * width)
    return pl.pallas_call(
        functools.partial(ffn_kernel, sources, sizes),
        out_shape=[jax.ShapeDtypeStruct((size, width), BF) for size in sizes],
        in_specs=[pl.BlockSpec(memory_space=pl.ANY)] * len(held)
        + [pl.BlockSpec(memory_space=pltpu.VMEM)] * 3,
        out_specs=[pl.BlockSpec(memory_space=pl.ANY)] * n,
        scratch_shapes=[
            pltpu.VMEM((total, width), BF),
            pltpu.VMEM((total, hidden), BF),
            pltpu.VMEM((total, width), BF),
            pltpu.SemaphoreType.DMA((n,)),
            pltpu.SemaphoreType.DMA((n,)),
        ],
        compiler_params=pltpu.CompilerParams(vmem_limit_bytes=32 * 2**20),
        cost_estimate=pl.CostEstimate(
            flops=6 * total * width * hidden, bytes_accessed=moved, transcendentals=total * hidden
        ),
    )(*held, gate, up, down)


def cat(*pieces):
    return jnp.concatenate(pieces, axis=0)


def gather_compute_reduce(rows, gate, up, down, hidden_own):
    a, b = rows[:16], rows[16:]
    am, ap, a2 = shift_x(a, 1), shift_x(a, -1), shift_x(a, 2)
    b1m, b1p = shift_z(b, 1), shift_z(b, -1)
    am, ap, a2, b1m, b1p = lax.optimization_barrier((am, ap, a2, b1m, b1p))
    a0 = cat(a, am, ap, a2)
    zm, zp = shift_z(cat(a0, b1m), 1), shift_z(cat(b1p, a0), -1)
    x1 = cat(b, b1m, b1p)
    x1m, x1p = shift_x(x1, 1), shift_x(x1, -1)
    zm, zp, x1m, x1p, hidden_own = lax.optimization_barrier((zm, zp, x1m, x1p, hidden_own))
    z1m, z1p = zm, zp
    zm, zp = shift_z(z1m, 1), shift_z(z1p, -1)
    x2 = cat(z1m[64:], z1p[:32])
    x2m, x2p = shift_x(cat(x2, x1m[:48]), 1), shift_x(cat(x2, x1p[48:]), -1)
    out_1 = ffn(
        (a0, (z1m, 0, 64), (z1p, 32, 64), x1, x1m, x1p), gate, up, down
    )
    z2m, z2p = zm, zp
    z2m, z2p, x2m, x2p, out_1 = lax.optimization_barrier((z2m, z2p, x2m, x2p, out_1))
    hidden_own = hidden_own.transpose(1, 0, 2).reshape(hidden_own.shape[1], -1)
    zm, zp = shift_z(z2m[:80], 1), shift_z(z2p[16:], -1)
    x3 = cat(z2m[64:], z2p[:32])
    x3m, x3p = shift_x(cat(x3, x2m[:32]), 1), shift_x(cat(x3, x2p[32:64]), -1)
    out_2 = ffn(
        (
            (z2m, 0, 64),
            (z2p, 32, 64),
            x2,
            (x2m, 0, 64),
            (x2p, 0, 64),
            (x2m, 64, 48),
            (x2p, 64, 48),
        ),
        gate,
        up,
        down,
    )
    z3m, z3p = zm, zp
    z3m, z3p, x3m, x3p, out_2 = lax.optimization_barrier((z3m, z3p, x3m, x3p, out_2))
    z4m, z4p = shift_z(z3m[:32], 1), shift_z(z3p[48:], -1)
    x4 = cat(z3m[64:], z3p[:16])
    x4m = shift_x(cat(x4, x3m[:32], out_2[6]), 1)
    x4p = shift_x(cat(x4, x3p[32:64], out_2[5]), -1)
    out_3 = ffn(
        (
            (z3m, 0, 64),
            (z3p, 16, 64),
            x4,
            x3,
            x3m,
            x3p,
        ),
        gate,
        up,
        down,
    )
    z4m, z4p, x4m, x4p, out_3 = lax.optimization_barrier((z4m, z4p, x4m, x4p, out_3))
    x5m, x5p = shift_x(x4m[:16], 1), shift_x(x4p[16:32], -1)
    out_4 = ffn((z4m, z4p, (x4m, 0, 64), (x4p, 0, 64)), gate, up, down)
    h1m, h1p = x4p[64:], x4m[64:]
    x5m, x5p, out_4 = lax.optimization_barrier((x5m, x5p, out_4))
    out_5 = ffn((x5m, x5p), gate, up, down)

    a0, a1m, a1p, x1, x1m, x1p = out_1
    a2m, a2p, x2, x2m, x2p = out_2[:5]
    a3m, a3p, x4, x3, x3m, x3p = out_3
    a4m, a4p, x4m, x4p = out_4
    x5m, x5p = out_5
    zm, zp = shift_z(a4m, -1), shift_z(a4p, 1)
    xm, xp = shift_x(x5m, -1), shift_x(x5p, 1)
    x1m, x1p = added(96, (x1m, 0), (h1m, 0)), added(96, (x1p, 0), (h1p, 48))
    zm = shift_z(added(64, (a3m, 0), (zm, 0)), -1)
    zp = shift_z(added(64, (a3p, 0), (zp, 32)), 1)
    xm = shift_x(added(64, (x4m, 0), (xm, 0)), -1)
    xp = shift_x(added(64, (x4p, 0), (xp, 16)), 1)
    b4 = added(32, (x4, 0), (xm[:32], 0), (xp[:32], 0))
    zm = shift_z(added(80, (a2m, 0), (zm, 0), (b4[:16], 64)), -1)
    zp = shift_z(added(80, (a2p, 16), (zp, 16), (b4[16:], 0)), 1)
    xm = shift_x(added(96, (x3m, 0), (xm[32:], 0)), -1)
    xp = shift_x(added(96, (x3p, 0), (xp[32:], 32)), 1)
    b3 = added(64, (x3, 0), (xm[:64], 0), (xp[:64], 0))
    zm = shift_z(added(96, (a1m, 0), (zm, 0), (b3[:32], 64)), -1)
    zp = shift_z(added(96, (a1p, 32), (zp, 16), (b3[32:], 0)), 1)
    xm = shift_x(added(96, (x2m, 0), (xm[64:], 0), (x1m[:32], 64)), -1)
    xp = shift_x(added(96, (x2p, 0), (xp[64:], 32), (x1p[:32], 64)), 1)
    b2 = added(64, (x2, 0), (xm[:64], 0), (xp[:64], 0))
    b = added(32, (x1[:32], 0), (xm[64:], 0), (xp[64:], 0))
    a = added(64, (a0, 0), (zm[:64], 0), (zp[32:], 0))
    zm = shift_z(added(32, (b2[:32], 0), (zm[64:], 0)), -1)
    zp = shift_z(added(32, (b2[32:], 0), (zp[:32], 0)), 1)
    xm, xp = shift_x(cat(x1m[32:], a[16:32]), -1), shift_x(cat(x1p[32:], a[32:48]), 1)
    a2 = shift_x(a[48:], 2)
    b1 = added(64, (x1[32:], 0), (xm[:64], 0), (xp[:64], 0))
    zm = shift_z(added(32, (b1[:32], 0), (zm, 0)), -1)
    zp = shift_z(added(32, (b1[32:], 0), (zp, 0)), 1)
    a_sum = added(16, (a[:16], 0), (xm[64:], 0), (xp[64:], 0), (a2, 0))
    b_sum = added(32, (b, 0), (zm, 0), (zp, 0))
    return (a_sum, b_sum), hidden_own


def parts_of_log(total):
    first = lax.reduce_precision(total, 8, 7)
    second = lax.reduce_precision(total - first, 8, 7)
    third = total - first - second
    return first.astype(BF), second.astype(BF), third.astype(BF)


def carried_state(block_total, block_state):
    heads = block_total.shape[0]
    seqs = lax.axis_size("seq")
    state = block_state.astype(BF).reshape(seqs, -1, 128)
    each = state.shape[1]
    marks = jnp.stack(parts_of_log(block_total), axis=0)
    marks = jnp.repeat(marks, seqs // heads, axis=1).T
    marks = jnp.broadcast_to(marks[:, :, None], (seqs, 3, 128))
    marks = jnp.concatenate([marks, jnp.zeros((seqs, 5, 128), BF)], axis=1)
    sent = jnp.concatenate([state, marks], axis=1)
    got = lax.all_to_all(sent, "seq", split_axis=0, concat_axis=0, tiled=True)
    totals = jnp.sum(got[:, each : each + 3, 0].astype(F32), axis=1)
    row = lax.broadcasted_iota(jnp.int32, (seqs, seqs), 0)
    col = lax.broadcasted_iota(jnp.int32, (seqs, seqs), 1)
    upto = jnp.sum(jnp.where(row >= col, totals[None, :], 0.0), axis=1)
    before = upto - totals
    gap = jnp.where(row > col, before[:, None] - upto[None, :], 0.0)
    weight = jnp.where(row > col, jnp.exp(gap), 0.0)
    states = got[:, :each, :].reshape(seqs, -1).astype(F32)
    summed = jnp.dot(weight, states, precision=lax.Precision.HIGHEST).astype(BF)
    back = lax.all_to_all(
        summed.reshape(seqs, each, 128), "seq", split_axis=0, concat_axis=0, tiled=True
    )
    return back.reshape(heads, 128, 128)


def route_targets(ids_block, experts):
    flat_ids = ids_block.reshape(-1)
    onehot = (flat_ids[:, None] == jnp.arange(experts, dtype=jnp.int32)[None, :]).astype(F32)
    n = flat_ids.shape[0]
    earlier = (jnp.arange(n)[:, None] > jnp.arange(n)[None, :]).astype(F32)
    before = jnp.dot(earlier, onehot, preferred_element_type=F32)
    slot = jnp.sum(before * onehot, axis=1).astype(jnp.int32)
    return flat_ids * CAP + slot


def body(
    queries,
    keys,
    values,
    log_decay,
    residual,
    attn_gain,
    moe_gain,
    expert_ids,
    gate_weights,
    w_gate,
    w_up,
    w_down,
):
    rows = queries.shape[0]
    heads = log_decay.shape[1]
    hd = queries.shape[1] // heads
    exps = lax.axis_size("exp")
    tok_rows, width = residual.shape
    share = width // exps
    place = lax.axis_index("exp")

    slots = exps * CAP
    target = route_targets(expert_ids, exps).reshape(tok_rows, 2)
    marked = jnp.concatenate(
        [
            residual.reshape(tok_rows, exps, share).transpose(1, 0, 2),
            jnp.broadcast_to(
                jnp.pad(target.astype(BF), ((0, 0), (0, 126)))[None], (exps, tok_rows, 128)
            ),
        ],
        axis=2,
    )
    block_tokens = butterfly(marked, "exp")
    block_tokens = block_tokens.reshape(exps * tok_rows, share + 128)
    res_cols = block_tokens[:, :share]
    targets = block_tokens[:, share : share + 2].astype(jnp.int32).reshape(exps, tok_rows, 2)
    gain_cols = lax.dynamic_slice_in_dim(attn_gain, place * share, share, axis=0)

    q_heads = queries.reshape(rows, heads, hd)
    k_heads = keys.reshape(rows, heads, hd)
    v_heads = values.reshape(rows, heads, hd)
    causal = lax.broadcasted_iota(jnp.int32, (rows, rows), 0) >= lax.broadcasted_iota(
        jnp.int32, (rows, rows), 1
    )
    log_cum = jnp.dot(causal.astype(F32), log_decay, precision=lax.Precision.HIGHEST)
    block_total = log_cum[-1]
    keys_weighted = (k_heads * jnp.exp(block_total[None, :] - log_cum)[:, :, None]).astype(BF)
    block_state = jnp.einsum("thd,the->hde", keys_weighted, v_heads, preferred_element_type=F32)
    carried = carried_state(block_total, block_state)
    scores = jnp.einsum("thd,shd->hts", q_heads, k_heads, preferred_element_type=F32)
    gap_logs = log_cum.T[:, :, None] - log_cum.T[:, None, :]
    mask = causal[None, :, :]
    weights = jnp.where(mask, scores * jnp.exp(jnp.where(mask, gap_logs, 0.0)), 0.0).astype(BF)
    intra = jnp.einsum("hts,she->the", weights, v_heads, preferred_element_type=F32)
    inter = jnp.exp(log_cum)[:, :, None] * jnp.einsum(
        "thd,hde->the", q_heads, carried, preferred_element_type=F32
    )
    attn = intra + inter
    normed = (attn * lax.rsqrt(jnp.mean(attn * attn, axis=-1, keepdims=True) + 1e-06)).astype(BF)
    normed = normed.reshape(rows, heads * hd)
    hidden_cols = (res_cols.astype(F32) + normed.astype(F32) * gain_cols[None, :]).astype(BF)

    slot_range = jnp.arange(slots, dtype=jnp.int32)
    hit = jnp.any(targets[:, None, :, :] == slot_range[None, :, None, None], axis=3)
    picker = hit.astype(BF)
    outgoing = jnp.einsum(
        "jkt,jtd->kjd",
        picker,
        hidden_cols.reshape(exps, tok_rows, share),
        preferred_element_type=F32,
    ).astype(BF)
    outgoing = outgoing.reshape(exps, CAP * exps, share)
    outgoing, hidden_cols = lax.optimization_barrier((outgoing, hidden_cols))
    arrived = lax.all_to_all(outgoing, "exp", split_axis=0, concat_axis=0, tiled=True)
    hidden_own = butterfly(hidden_cols.reshape(exps, tok_rows, share), "exp")
    hid_rows = arrived.transpose(1, 0, 2).reshape(slots, width)
    hid32_rows = hid_rows.astype(F32)
    moe_rows = (
        hid32_rows
        * lax.rsqrt(jnp.mean(hid32_rows * hid32_rows, axis=-1, keepdims=True) + 1e-06)
        * moe_gain
    ).astype(BF)

    expert_sums, hidden_own = gather_compute_reduce(
        moe_rows, w_gate[0], w_up[0], w_down[0], hidden_own
    )
    expert_rows = jnp.concatenate(expert_sums, axis=0).astype(BF)

    by_block = expert_rows.reshape(CAP, exps, width).transpose(1, 0, 2)
    returned = lax.all_to_all(by_block, "exp", split_axis=0, concat_axis=0, tiled=True)
    flat_back = returned.reshape(slots, width)
    chosen = (target[:, :, None] == slot_range[None, None, :]).astype(BF)
    picked = jnp.einsum("trk,kd->trd", chosen, flat_back, preferred_element_type=F32)
    mixed = hidden_own.astype(F32) + jnp.sum(gate_weights[:, :, None] * picked, axis=1)
    return mixed.astype(BF)


def solution(mesh):
    in_specs = (
        P("seq", "exp"),
        P("seq", "exp"),
        P("seq", "exp"),
        P("seq", "exp"),
        P(("seq", "exp"), None),
        P(),
        P(),
        P(("seq", "exp"), None),
        P(("seq", "exp"), None),
        P("exp", "seq", None),
        P("exp", "seq", None),
        P("exp", "seq", None),
    )
    out_specs = P(("seq", "exp"), None)
    return jax.shard_map(body, mesh=mesh, in_specs=in_specs, out_specs=out_specs, check_vma=False)
```

```python
import functools

import jax
import jax.numpy as jnp
from jax import lax
from jax.experimental import pallas as pl
from jax.experimental.pallas import tpu as pltpu
from jax.sharding import PartitionSpec as P

BF = jnp.bfloat16
F32 = jnp.float32
NX, NZ = 4, 8
CAP = 6


def shift_x(value, by):
    pairs = [(x * NZ + z, ((x + by) % NX) * NZ + z) for x in range(NX) for z in range(NZ)]
    return lax.ppermute(value, "seq", pairs)


def shift_z(value, by):
    pairs = [(x * NZ + z, x * NZ + (z + by) % NZ) for x in range(NX) for z in range(NZ)]
    return lax.ppermute(value, "seq", pairs)


def butterfly(blocks, axis):
    n = blocks.shape[0]
    place = lax.axis_index(axis)
    step = 1
    while step < n:
        split = blocks.reshape((n // (2 * step), 2, step) + blocks.shape[1:])
        low, high = split[:, 0], split[:, 1]
        upper = (place // step) % 2 == 1
        got = lax.ppermute(jnp.where(upper, low, high), axis, [(i, i ^ step) for i in range(n)])
        low, high = jnp.where(upper, got, low), jnp.where(upper, high, got)
        blocks = jnp.stack([low, high], axis=1).reshape(blocks.shape)
        step *= 2
    return blocks


def added(rows, *parts):
    total = 0.0
    for part, at in parts:
        after = rows - at - part.shape[0]
        total = total + jnp.pad(part.astype(F32), ((at, after), (0, 0)))
    return total.astype(BF)


def ffn_kernel(sources, sizes, *refs):
    n, given = len(sizes), max(which for which, _ in sources) + 1
    held, (gate, up, down) = refs[:given], refs[given : given + 3]
    outs = refs[given + 3 : given + 3 + n]
    x, active, y, sem_x, sem_y = refs[given + 3 + n :]
    pieces = [held[which].at[pl.ds(at, size)] for (which, at), size in zip(sources, sizes)]
    hidden, width = gate.shape
    main = hidden // 256 * 256
    starts = [sum(sizes[:i]) for i in range(n)]
    loads = [
        pltpu.make_async_copy(pieces[i], x.at[pl.ds(starts[i], sizes[i])], sem_x.at[i])
        for i in range(n)
    ]
    for copy in loads:
        copy.start()
    for copy in loads:
        copy.wait()

    def product(rows, block):
        return lax.dot_general(
            rows, block, (((1,), (1,)), ((), ())), preferred_element_type=F32
        )

    g = product(x[...], gate[:main, :])
    u = product(x[...], up[:main, :])
    active[:, :main] = (g / (1.0 + jnp.exp(-g)) * u).astype(BF)
    rest = product(x[...], jnp.concatenate([gate[main:, :], up[main:, :]], axis=0))
    g, u = rest[:, : hidden - main], rest[:, hidden - main :]
    active[:, main:] = (g / (1.0 + jnp.exp(-g)) * u).astype(BF)
    step = 512

    @pl.loop(0, width // step)
    def _(j):
        cols = pl.ds(pl.multiple_of(j * step, step), step)
        y[:, cols] = jnp.dot(active[...], down[:, cols], preferred_element_type=F32).astype(BF)

    stores = [
        pltpu.make_async_copy(y.at[pl.ds(starts[i], sizes[i])], outs[i], sem_y.at[i])
        for i in range(n)
    ]
    for copy in stores:
        copy.start()
    for copy in stores:
        copy.wait()


def ffn(pieces, gate, up, down):
    held, sources, sizes = [], [], []
    for piece in pieces:
        array, at, size = piece if isinstance(piece, tuple) else (piece, 0, piece.shape[0])
        if not any(array is other for other in held):
            held.append(array)
        sources.append(([array is other for other in held].index(True), at))
        sizes.append(size)
    total, n = sum(sizes), len(sizes)
    hidden, width = gate.shape
    moved = 2 * (2 * total * width + 3 * hidden * width)
    return pl.pallas_call(
        functools.partial(ffn_kernel, sources, sizes),
        out_shape=[jax.ShapeDtypeStruct((size, width), BF) for size in sizes],
        in_specs=[pl.BlockSpec(memory_space=pl.ANY)] * len(held)
        + [pl.BlockSpec(memory_space=pltpu.VMEM)] * 3,
        out_specs=[pl.BlockSpec(memory_space=pl.ANY)] * n,
        scratch_shapes=[
            pltpu.VMEM((total, width), BF),
            pltpu.VMEM((total, hidden), BF),
            pltpu.VMEM((total, width), BF),
            pltpu.SemaphoreType.DMA((n,)),
            pltpu.SemaphoreType.DMA((n,)),
        ],
        compiler_params=pltpu.CompilerParams(vmem_limit_bytes=32 * 2**20),
        cost_estimate=pl.CostEstimate(
            flops=6 * total * width * hidden, bytes_accessed=moved, transcendentals=total * hidden
        ),
    )(*held, gate, up, down)


def cat(*pieces):
    return jnp.concatenate(pieces, axis=0)


def gather_compute_reduce(rows, gate, up, down, hidden_own):
    a, b = rows[:16], rows[16:]
    am, ap, a2 = shift_x(a, 1), shift_x(a, -1), shift_x(a, 2)
    b1m, b1p = shift_z(b, 1), shift_z(b, -1)
    am, ap, a2, b1m, b1p = lax.optimization_barrier((am, ap, a2, b1m, b1p))
    a0 = cat(a, am, ap, a2)
    zm, zp = shift_z(cat(a0, b1m), 1), shift_z(cat(b1p, a0), -1)
    x1 = cat(b, b1m, b1p)
    x1m, x1p = shift_x(x1, 1), shift_x(x1, -1)
    zm, zp, x1m, x1p, hidden_own = lax.optimization_barrier((zm, zp, x1m, x1p, hidden_own))
    z1m, z1p = zm, zp
    zm, zp = shift_z(z1m, 1), shift_z(z1p, -1)
    x2 = cat(z1m[64:], z1p[:32])
    x2m, x2p = shift_x(cat(x2, x1m[:48]), 1), shift_x(cat(x2, x1p[48:]), -1)
    out_1 = ffn(
        (a0, (z1m, 0, 64), (z1p, 32, 64), x1, x1m, x1p), gate, up, down
    )
    z2m, z2p = zm, zp
    z2m, z2p, x2m, x2p, out_1 = lax.optimization_barrier((z2m, z2p, x2m, x2p, out_1))
    hidden_own = hidden_own.transpose(1, 0, 2).reshape(hidden_own.shape[1], -1)
    zm, zp = shift_z(z2m[:80], 1), shift_z(z2p[16:], -1)
    x3 = cat(z2m[64:], z2p[:32])
    x3m, x3p = shift_x(cat(x3, x2m[:32]), 1), shift_x(cat(x3, x2p[32:64]), -1)
    out_2 = ffn(
        (
            (z2m, 0, 64),
            (z2p, 32, 64),
            x2,
            (x2m, 0, 64),
            (x2p, 0, 64),
            (x2m, 64, 48),
            (x2p, 64, 48),
        ),
        gate,
        up,
        down,
    )
    z3m, z3p = zm, zp
    z3m, z3p, x3m, x3p, out_2 = lax.optimization_barrier((z3m, z3p, x3m, x3p, out_2))
    z4m, z4p = shift_z(z3m[:32], 1), shift_z(z3p[48:], -1)
    x4 = cat(z3m[64:], z3p[:16])
    x4m = shift_x(cat(x4, x3m[:32], out_2[6]), 1)
    x4p = shift_x(cat(x4, x3p[32:64], out_2[5]), -1)
    out_3 = ffn(
        (
            (z3m, 0, 64),
            (z3p, 16, 64),
            x4,
            x3,
            x3m,
            x3p,
        ),
        gate,
        up,
        down,
    )
    z4m, z4p, x4m, x4p, out_3 = lax.optimization_barrier((z4m, z4p, x4m, x4p, out_3))
    x5m, x5p = shift_x(x4m[:16], 1), shift_x(x4p[16:32], -1)
    out_4 = ffn((z4m, z4p, (x4m, 0, 64), (x4p, 0, 64)), gate, up, down)
    h1m, h1p = x4p[64:], x4m[64:]
    x5m, x5p, out_4 = lax.optimization_barrier((x5m, x5p, out_4))
    out_5 = ffn((x5m, x5p), gate, up, down)

    a0, a1m, a1p, x1, x1m, x1p = out_1
    a2m, a2p, x2, x2m, x2p = out_2[:5]
    a3m, a3p, x4, x3, x3m, x3p = out_3
    a4m, a4p, x4m, x4p = out_4
    x5m, x5p = out_5
    zm, zp = shift_z(a4m, -1), shift_z(a4p, 1)
    xm, xp = shift_x(x5m, -1), shift_x(x5p, 1)
    x1m, x1p = added(96, (x1m, 0), (h1m, 0)), added(96, (x1p, 0), (h1p, 48))
    zm = shift_z(added(64, (a3m, 0), (zm, 0)), -1)
    zp = shift_z(added(64, (a3p, 0), (zp, 32)), 1)
    xm = shift_x(added(64, (x4m, 0), (xm, 0)), -1)
    xp = shift_x(added(64, (x4p, 0), (xp, 16)), 1)
    b4 = added(32, (x4, 0), (xm[:32], 0), (xp[:32], 0))
    zm = shift_z(added(80, (a2m, 0), (zm, 0), (b4[:16], 64)), -1)
    zp = shift_z(added(80, (a2p, 16), (zp, 16), (b4[16:], 0)), 1)
    xm = shift_x(added(96, (x3m, 0), (xm[32:], 0)), -1)
    xp = shift_x(added(96, (x3p, 0), (xp[32:], 32)), 1)
    b3 = added(64, (x3, 0), (xm[:64], 0), (xp[:64], 0))
    xm = added(96, (x2m, 0), (xm[64:], 0), (x1m[:32], 64))
    xp = added(96, (x2p, 0), (xp[64:], 32), (x1p[:32], 64))
    xm, xp, b3 = lax.optimization_barrier((xm, xp, b3))
    xm, xp = shift_x(xm, -1), shift_x(xp, 1)
    zm = shift_z(added(96, (a1m, 0), (zm, 0), (b3[:32], 64)), -1)
    zp = shift_z(added(96, (a1p, 32), (zp, 16), (b3[32:], 0)), 1)
    b2 = added(64, (x2, 0), (xm[:64], 0), (xp[:64], 0))
    b = added(32, (x1[:32], 0), (xm[64:], 0), (xp[64:], 0))
    a = added(64, (a0, 0), (zm[:64], 0), (zp[32:], 0))
    zm = shift_z(added(32, (b2[:32], 0), (zm[64:], 0)), -1)
    zp = shift_z(added(32, (b2[32:], 0), (zp[:32], 0)), 1)
    xm, xp = shift_x(cat(x1m[32:], a[16:32]), -1), shift_x(cat(x1p[32:], a[32:48]), 1)
    a2 = shift_x(a[48:], 2)
    b1 = added(64, (x1[32:], 0), (xm[:64], 0), (xp[:64], 0))
    zm = shift_z(added(32, (b1[:32], 0), (zm, 0)), -1)
    zp = shift_z(added(32, (b1[32:], 0), (zp, 0)), 1)
    a_sum = added(16, (a[:16], 0), (xm[64:], 0), (xp[64:], 0), (a2, 0))
    b_sum = added(32, (b, 0), (zm, 0), (zp, 0))
    return (a_sum, b_sum), hidden_own


def parts_of_log(total):
    first = lax.reduce_precision(total, 8, 7)
    second = lax.reduce_precision(total - first, 8, 7)
    third = total - first - second
    return first.astype(BF), second.astype(BF), third.astype(BF)


def carried_state(block_total, block_state):
    heads = block_total.shape[0]
    seqs = lax.axis_size("seq")
    state = block_state.astype(BF).reshape(seqs, -1, 128)
    each = state.shape[1]
    marks = jnp.stack(parts_of_log(block_total), axis=0)
    marks = jnp.repeat(marks, seqs // heads, axis=1).T
    marks = jnp.broadcast_to(marks[:, :, None], (seqs, 3, 128))
    marks = jnp.concatenate([marks, jnp.zeros((seqs, 5, 128), BF)], axis=1)
    sent = jnp.concatenate([state, marks], axis=1)
    got = lax.all_to_all(sent, "seq", split_axis=0, concat_axis=0, tiled=True)
    totals = jnp.sum(got[:, each : each + 3, 0].astype(F32), axis=1)
    row = lax.broadcasted_iota(jnp.int32, (seqs, seqs), 0)
    col = lax.broadcasted_iota(jnp.int32, (seqs, seqs), 1)
    upto = jnp.sum(jnp.where(row >= col, totals[None, :], 0.0), axis=1)
    before = upto - totals
    gap = jnp.where(row > col, before[:, None] - upto[None, :], 0.0)
    weight = jnp.where(row > col, jnp.exp(gap), 0.0)
    states = got[:, :each, :].reshape(seqs, -1).astype(F32)
    summed = jnp.dot(weight, states, precision=lax.Precision.HIGHEST).astype(BF)
    back = lax.all_to_all(
        summed.reshape(seqs, each, 128), "seq", split_axis=0, concat_axis=0, tiled=True
    )
    return back.reshape(heads, 128, 128)


def route_targets(ids_block, experts):
    flat_ids = ids_block.reshape(-1)
    onehot = (flat_ids[:, None] == jnp.arange(experts, dtype=jnp.int32)[None, :]).astype(F32)
    n = flat_ids.shape[0]
    earlier = (jnp.arange(n)[:, None] > jnp.arange(n)[None, :]).astype(F32)
    before = jnp.dot(earlier, onehot, preferred_element_type=F32)
    slot = jnp.sum(before * onehot, axis=1).astype(jnp.int32)
    return flat_ids * CAP + slot


def body(
    queries,
    keys,
    values,
    log_decay,
    residual,
    attn_gain,
    moe_gain,
    expert_ids,
    gate_weights,
    w_gate,
    w_up,
    w_down,
):
    rows = queries.shape[0]
    heads = log_decay.shape[1]
    hd = queries.shape[1] // heads
    exps = lax.axis_size("exp")
    tok_rows, width = residual.shape
    share = width // exps
    place = lax.axis_index("exp")

    slots = exps * CAP
    target = route_targets(expert_ids, exps).reshape(tok_rows, 2)
    marked = jnp.concatenate(
        [
            residual.reshape(tok_rows, exps, share).transpose(1, 0, 2),
            jnp.broadcast_to(
                jnp.pad(target.astype(BF), ((0, 0), (0, 126)))[None], (exps, tok_rows, 128)
            ),
        ],
        axis=2,
    )
    block_tokens = butterfly(marked, "exp")
    block_tokens = block_tokens.reshape(exps * tok_rows, share + 128)
    res_cols = block_tokens[:, :share]
    targets = block_tokens[:, share : share + 2].astype(jnp.int32).reshape(exps, tok_rows, 2)
    gain_cols = lax.dynamic_slice_in_dim(attn_gain, place * share, share, axis=0)

    q_heads = queries.reshape(rows, heads, hd)
    k_heads = keys.reshape(rows, heads, hd)
    v_heads = values.reshape(rows, heads, hd)
    causal = lax.broadcasted_iota(jnp.int32, (rows, rows), 0) >= lax.broadcasted_iota(
        jnp.int32, (rows, rows), 1
    )
    log_cum = jnp.dot(causal.astype(F32), log_decay, precision=lax.Precision.HIGHEST)
    block_total = log_cum[-1]
    keys_weighted = (k_heads * jnp.exp(block_total[None, :] - log_cum)[:, :, None]).astype(BF)
    block_state = jnp.einsum("thd,the->hde", keys_weighted, v_heads, preferred_element_type=F32)
    carried = carried_state(block_total, block_state)
    scores = jnp.einsum("thd,shd->hts", q_heads, k_heads, preferred_element_type=F32)
    gap_logs = log_cum.T[:, :, None] - log_cum.T[:, None, :]
    mask = causal[None, :, :]
    weights = jnp.where(mask, scores * jnp.exp(jnp.where(mask, gap_logs, 0.0)), 0.0).astype(BF)
    intra = jnp.einsum("hts,she->the", weights, v_heads, preferred_element_type=F32)
    inter = jnp.exp(log_cum)[:, :, None] * jnp.einsum(
        "thd,hde->the", q_heads, carried, preferred_element_type=F32
    )
    attn = intra + inter
    normed = (attn * lax.rsqrt(jnp.mean(attn * attn, axis=-1, keepdims=True) + 1e-06)).astype(BF)
    normed = normed.reshape(rows, heads * hd)
    hidden_cols = (res_cols.astype(F32) + normed.astype(F32) * gain_cols[None, :]).astype(BF)

    slot_range = jnp.arange(slots, dtype=jnp.int32)
    hit = jnp.any(targets[:, None, :, :] == slot_range[None, :, None, None], axis=3)
    picker = hit.astype(BF)
    outgoing = jnp.einsum(
        "jkt,jtd->kjd",
        picker,
        hidden_cols.reshape(exps, tok_rows, share),
        preferred_element_type=F32,
    ).astype(BF)
    outgoing = outgoing.reshape(exps, CAP * exps, share)
    outgoing, hidden_cols = lax.optimization_barrier((outgoing, hidden_cols))
    arrived = lax.all_to_all(outgoing, "exp", split_axis=0, concat_axis=0, tiled=True)
    hidden_own = butterfly(hidden_cols.reshape(exps, tok_rows, share), "exp")
    hid_rows = arrived.transpose(1, 0, 2).reshape(slots, width)
    hid32_rows = hid_rows.astype(F32)
    moe_rows = (
        hid32_rows
        * lax.rsqrt(jnp.mean(hid32_rows * hid32_rows, axis=-1, keepdims=True) + 1e-06)
        * moe_gain
    ).astype(BF)

    expert_sums, hidden_own = gather_compute_reduce(
        moe_rows, w_gate[0], w_up[0], w_down[0], hidden_own
    )
    expert_rows = jnp.concatenate(expert_sums, axis=0).astype(BF)

    by_block = expert_rows.reshape(CAP, exps, width).transpose(1, 0, 2)
    returned = lax.all_to_all(by_block, "exp", split_axis=0, concat_axis=0, tiled=True)
    flat_back = returned.reshape(slots, width)
    chosen = (target[:, :, None] == slot_range[None, None, :]).astype(BF)
    picked = jnp.einsum("trk,kd->trd", chosen, flat_back, preferred_element_type=F32)
    mixed = hidden_own.astype(F32) + jnp.sum(gate_weights[:, :, None] * picked, axis=1)
    return mixed.astype(BF)


def solution(mesh):
    in_specs = (
        P("seq", "exp"),
        P("seq", "exp"),
        P("seq", "exp"),
        P("seq", "exp"),
        P(("seq", "exp"), None),
        P(),
        P(),
        P(("seq", "exp"), None),
        P(("seq", "exp"), None),
        P("exp", "seq", None),
        P("exp", "seq", None),
        P("exp", "seq", None),
    )
    out_specs = P(("seq", "exp"), None)
    return jax.shard_map(body, mesh=mesh, in_specs=in_specs, out_specs=out_specs, check_vma=False)
```
